512 devices in a mesh: tm: 16 (over y, x_hi), space: 32 (over z, x_lo, core).
Axes of the slice: x: 4 (x_hi: 2, x_lo: 2; x = x_hi * 2 + x_lo), y: 8, z: 8, core: 2. Of those that a mesh axis runs over, the one named last changes fastest.
Arguments:
- states: float32 [16, 3, 2, 128, 128, 128], P('tm', None, None, 'space'), may hold values from 0 to 1
- first_start: float32 [2, 128, 128, 128], P(None, 'space'), may hold values from 0 to 1
Outputs:
- next_states: float32 [16, 3, 2, 128, 128, 128], P('tm', None, None, 'space')
The draws below stay inside these ranges and needn't reach their ends.
All inputs are finite; a program needn't handle non-finite values.
Results may differ from the reference program's by a relative error of at most 0.00002.
Values sent between devices are 32-bit elements; how exact they have to be, the bound alone decides.
No kernel may reach another device: no remote copies, remote signals or barrier semaphores. Data moves between devices by JAX's collectives and lax.ppermute only.
A program may use at most 64 MiB of HBM per device.

```python
import jax
import jax.numpy as jnp

NY = 128
NZ = 128
NODES = 3
FIELDS = 2
NX = 128
SLABS = 16


def steps_of(rng, dims, cuts, low, high):
    gain = 1.0
    for dim, shards_of in cuts:
        steps = jax.random.uniform(jax.random.fold_in(jax.random.fold_in(rng, 6), dim), (shards_of,), jnp.float32, low / len(cuts), high / len(cuts))
        gain = gain * jnp.repeat(jnp.exp(steps), dims[dim] // shards_of).reshape((-1,) + (1,) * (len(dims) - 1 - dim))
    return gain


def setup_inputs(seed: int = 0) -> dict:
    splits = jax.random.split(jax.random.key(seed), 3)
    return {
        "states": jnp.clip(1.0 * jax.random.uniform(splits[0], (SLABS, NODES, FIELDS, NX, NY, NZ), jnp.float32) ** steps_of(splits[0], (SLABS, NODES, FIELDS, NX, NY, NZ), ((0, 16), (3, 32)), -0.2, 0.2), 0.0, 1.0),
        "first_start": jnp.clip(1.0 * jax.random.uniform(splits[1], (FIELDS, NX, NY, NZ), jnp.float32) ** steps_of(splits[1], (FIELDS, NX, NY, NZ), ((1, 32),), -0.2, 0.2), 0.0, 1.0),
    }


step_time = 0.25
half_step = 0.125
diffuse_fast = 0.6
diffuse_slow = 0.3
feed_rate = 0.04
kill_rate = 0.06


def laplace_sum(field):
    total = jnp.roll(field, -1, -3) + jnp.roll(field, 1, -3)
    total = total + jnp.roll(field, 1, -2) + jnp.roll(field, -1, -2)
    total = total + jnp.roll(field, 1, -1) + jnp.roll(field, -1, -1)
    return total - 6.0 * field


def reaction_rates(state):
    substrate = state[..., 0, :, :, :]
    catalyst = state[..., 1, :, :, :]
    product = substrate * catalyst * catalyst
    rate_sub = diffuse_fast * laplace_sum(substrate) - product + feed_rate * (1.0 - substrate)
    rate_cat = diffuse_slow * laplace_sum(catalyst) + product - (feed_rate + kill_rate) * catalyst
    return jnp.stack([rate_sub, rate_cat], axis=-4)


def reference(states, first_start):
    previous = reaction_rates(states)
    old_zero, old_one, old_two = previous[:, 0], previous[:, 1], previous[:, 2]
    slab_start = jnp.concatenate([first_start[None], states[:-1, 2]], axis=0)
    rate_zero = reaction_rates(slab_start)
    fine_one = slab_start + half_step * (rate_zero - old_zero) + step_time * (5.0 / 24.0 * old_zero + 1.0 / 3.0 * old_one - 1.0 / 24.0 * old_two)
    rate_one = reaction_rates(fine_one)
    fine_two = fine_one + half_step * (rate_one - old_one) + step_time * (-1.0 / 24.0 * old_zero + 1.0 / 3.0 * old_one + 5.0 / 24.0 * old_two)
    rate_two = reaction_rates(fine_two)
    offset = step_time * 0.5 * (rate_two - rate_zero) + step_time * (2.0 / 3.0 * rate_one - 1.0 / 3.0 * rate_zero - 1.0 / 3.0 * rate_two)
    starts = []
    ends = []
    coarse_start = first_start
    for slab in range(SLABS):
        if slab > 0:
            coarse_start = ends[-1]
        coarse_end = coarse_start + step_time * reaction_rates(coarse_start) + offset[slab]
        starts.append(coarse_start)
        ends.append(coarse_end)
    start_all = jnp.stack(starts)
    end_all = jnp.stack(ends)
    middle = fine_one + 0.5 * ((start_all - slab_start) + (end_all - fine_two))
    updated = jnp.stack([start_all, middle, end_all], axis=1)
    newest = jnp.stack([end_all[-1], end_all[-1], end_all[-1]])
    return jnp.concatenate([updated[1:], newest[None]], axis=0)
```

```python
import functools

import jax
import jax.numpy as jnp
from jax import lax
from jax.experimental import pallas as pl
from jax.experimental.pallas import tpu as pltpu
from jax.sharding import PartitionSpec as P

step_time = 0.25
half_step = 0.125
diffuse = (0.6, 0.3)
feed_rate = 0.04
kill_rate = 0.06
sweep_weights = ((5.0 / 24.0, 1.0 / 3.0, -1.0 / 24.0), (-1.0 / 24.0, 1.0 / 3.0, 5.0 / 24.0))
old_weights = (
    (step_time * 5.0 / 24.0 - half_step, step_time / 3.0, -step_time / 24.0),
    (-step_time / 24.0, step_time / 3.0 - half_step, step_time * 5.0 / 24.0),
)
new_weights = (
    -0.5 * step_time - step_time / 3.0,
    step_time * 2.0 / 3.0,
    0.5 * step_time - step_time / 3.0,
)
rows_each = 8
block_len = 4
half_rows = 4
vmem_bytes = 16 * 1024 * 1024


def rank_of(index, count):
    return index // 2 if index % 2 == 0 else count - 1 - index // 2


def index_of(rank, count):
    return 2 * rank if rank < count // 2 else 2 * (count - 1 - rank) + 1


def chain_blocks(count):
    blocks, first = [], 1
    while first < count:
        steps = min(block_len, count - first)
        blocks.append((first, steps, len(blocks) % 2))
        first += steps
    return blocks


even, last, offset_moved, end_moved = range(4)


def kind_of(slab):
    return jnp.where(slab > 0, ((slab - 1) // block_len) & 1, 2)


def flag(flags_ref, which, like):
    return jnp.broadcast_to(flags_ref[which : which + 1, :], like.shape) != 0


def call(kernel, out_shapes, *args):
    size = sum(4 * a.size for a in args) + sum(4 * o.size for o in out_shapes)
    return pl.pallas_call(
        kernel,
        out_shape=tuple(out_shapes),
        in_specs=[pl.BlockSpec(memory_space=pltpu.VMEM)] * len(args),
        out_specs=tuple(pl.BlockSpec(memory_space=pltpu.VMEM) for _ in out_shapes),
        compiler_params=pltpu.CompilerParams(vmem_limit_bytes=vmem_bytes),
        cost_estimate=pl.CostEstimate(flops=10 * size, bytes_accessed=size, transcendentals=0),
    )(*args)


def shape(*dims):
    return jax.ShapeDtypeStruct(dims, jnp.float32)


def plane_sum(x):
    rows, cols = x.shape[-2], x.shape[-1]
    total = pltpu.roll(x, 1, x.ndim - 2) + pltpu.roll(x, rows - 1, x.ndim - 2)
    total = total + pltpu.roll(x, 1, x.ndim - 1) + pltpu.roll(x, cols - 1, x.ndim - 1)
    return total - 6.0 * x


def reactions(s, c):
    product = s * c * c
    return feed_rate * (1.0 - s) - product, product - (feed_rate + kill_rate) * c


def plane_rates(lo, middle, hi):
    lap = [plane_sum(middle[f]) + lo[f] + hi[f] for f in range(2)]
    react = reactions(*middle)
    return [diffuse[f] * lap[f] + react[f] for f in range(2)]


def put_edges(flags_ref, far_ref, near_ref, at, head, tail):
    here = flag(flags_ref, even, head)
    far_ref[at] = jnp.where(here, head, tail)
    near_ref[at] = jnp.where(here, tail, head)


def below(flags_ref, far, near):
    return jnp.where(flag(flags_ref, even, far), far, near)


def above(flags_ref, far, near):
    return jnp.where(flag(flags_ref, even, far), near, far)


def combined(states_ref, way, f, p):
    w = old_weights[way]
    return sum(w[j] * states_ref[j, f, p] for j in range(3))


def start_kernel(flags_ref, states_ref, first_ref, far_ref, near_ref):
    sides = (0, states_ref.shape[2] - 1)
    for f in range(2):
        for way in range(2):
            put_edges(flags_ref, far_ref, near_ref, (way, f), *[combined(states_ref, way, f, p) for p in sides])
        ends = [states_ref[2, f, p] for p in sides]
        ends = [jnp.where(flag(flags_ref, last, x), first_ref[f, p], x) for p, x in zip(sides, ends)]
        put_edges(flags_ref, far_ref, near_ref, (2, f), *ends)


def old_kernel(flags_ref, states_ref, first_ref, part_ref, start_ref):
    depth = states_ref.shape[2]
    for p in range(depth):
        for f in range(2):
            own = states_ref[2, f, p]
            start_ref[f, p] = jnp.where(flag(flags_ref, last, own), first_ref[f, p], own)
        react = [reactions(states_ref[j, 0, p], states_ref[j, 1, p]) for j in range(3)]
        for way in range(2):
            for f in range(2):
                middle = combined(states_ref, way, f, p)
                total = plane_sum(middle)
                if p > 0:
                    total = total + combined(states_ref, way, f, p - 1)
                if p < depth - 1:
                    total = total + combined(states_ref, way, f, p + 1)
                part = diffuse[f] * total
                for j in range(3):
                    part = part + old_weights[way][j] * react[j][f]
                part_ref[way, f, p] = part


def sum_kernel(flags_ref, part_ref, far_ref, near_ref, *out_refs):
    depth = part_ref.shape[2]
    for way, out_ref in enumerate(out_refs):
        for f in range(2):
            for p in range(depth):
                total = part_ref[way, f, p]
                if p == 0:
                    total = total + diffuse[f] * below(flags_ref, far_ref[way, f], near_ref[way, f])
                if p == depth - 1:
                    total = total + diffuse[f] * above(flags_ref, far_ref[way, f], near_ref[way, f])
                out_ref[f, p] = total


def planes_with(flags_ref, x_ref, far_ref, near_ref):
    depth = x_ref.shape[1]

    def plane(p):
        if p < 0:
            return [below(flags_ref, far_ref[f], near_ref[f]) for f in range(2)]
        if p >= depth:
            return [above(flags_ref, far_ref[f], near_ref[f]) for f in range(2)]
        return [x_ref[f, p] for f in range(2)]

    return plane


def node_kernel(way, flags_ref, old_ref, x_ref, far_ref, near_ref, *refs):
    depth = x_ref.shape[1]
    plane = planes_with(flags_ref, x_ref, far_ref, near_ref)
    if way == 0:
        next_ref, keep_ref, next_far_ref, next_near_ref = refs
    else:
        rate_ref, next_ref, keep_ref, next_far_ref, next_near_ref = refs
    for p in range(depth):
        rate = plane_rates(plane(p - 1), plane(p), plane(p + 1))
        for f in range(2):
            next_ref[f, p] = x_ref[f, p] + half_step * rate[f] + old_ref[f, p]
            if way == 0:
                keep_ref[f, p] = rate[f]
            else:
                keep_ref[f, p] = new_weights[0] * rate_ref[f, p] + new_weights[1] * rate[f]
    for f in range(2):
        put_edges(flags_ref, next_far_ref, next_near_ref, f, next_ref[f, 0], next_ref[f, depth - 1])


def offset_kernel(
    count, planes, flags_ref, sum_ref, start_ref, node_ref, rate_ref, x_ref, *refs
):
    send_ref, offset_ref, mid_ref = refs[-3:]
    plane = planes_with(flags_ref, x_ref, *(refs[:2] if len(refs) > 3 else (None, None)))
    for q, p in enumerate(planes):
        rate = plane_rates(plane(p - 1), plane(p), plane(p + 1))
        for f in range(2):
            offset = sum_ref[f, p] + new_weights[2] * rate[f]
            offset_ref[f, q] = offset
            first = start_ref[f, p] + step_time * rate_ref[f, p] + offset
            offset = jnp.where(flag(flags_ref, last, offset), first, offset)
            moved = pltpu.roll(offset, half_rows, 0), pltpu.roll(offset, rows_each, 0)
            offset = jnp.where(flag(flags_ref, offset_moved, offset), *moved)
            offset = jnp.concatenate([offset, offset[:rows_each]], axis=0)
            for i in range(count):
                r = rank_of(i, count)
                send_ref[i, f, q] = offset[r * rows_each : (r + 2) * rows_each]
            mid_ref[f, q] = node_ref[f, p] - 0.5 * (start_ref[f, p] + x_ref[f, p])


def edge_lists(steps):
    return [(0, steps)] + [(j, steps - j) for j in range(1, steps)]


def joined(kind, own, come):
    return jnp.concatenate([come, own] if kind == 0 else [own, come], axis=-2)


def either(p, depth, inner, edges):
    return (inner, p - 1) if 0 < p < depth - 1 else (edges, min(p, 1))


def rows_of(kind, state, inner_ref, edges_ref):
    depth = inner_ref.shape[2] + 2

    def plane(a, f, p):
        if a:
            ref, q = either(p, depth, inner_ref, edges_ref)
            return ref[a - 1, f, q]
        if state[0].shape[2] == rows_each:
            return joined(kind, state[0][f, p], state[1][f, p])
        ref, q = either(p, depth, *state)
        return ref[f, q]

    return plane


def edge_kernel(kind, steps, flags_ref, inner_ref, edges_ref, *refs):
    far_ref, near_ref = refs[-2:]
    depth = inner_ref.shape[2] + 2
    plane = rows_of(kind, refs[:-2], inner_ref, edges_ref)
    at = 0
    for a, n in edge_lists(steps):
        for i in range(n):
            for f in range(2):
                put_edges(flags_ref, far_ref, near_ref, (f, at + i), plane(a, f, i), plane(a, f, depth - n + i))
        at += n


def block_kernel(kind, steps, flags_ref, inner_ref, edges_ref, *refs):
    far_ref, near_ref, out_ref, end_ref = refs[-4:]
    depth = inner_ref.shape[2] + 2
    plane = rows_of(kind, refs[:-4], inner_ref, edges_ref)
    at = {}
    place = 0
    for a, n in edge_lists(steps):
        at[a] = (place, n)
        place += n

    def extended(a, f):
        planes = [plane(a, f, p) for p in range(depth)]
        if a in at:
            place, n = at[a]
            halo = [(far_ref[f, place + i], near_ref[f, place + i]) for i in range(n)]
            lo = [below(flags_ref, *pair) for pair in halo]
            hi = [above(flags_ref, *pair) for pair in halo]
            planes = lo + planes + hi
        return jnp.stack(planes)

    state = [extended(0, f) for f in range(2)]
    for f in range(2):
        own = slice(rows_each, None) if kind == 0 else slice(None, rows_each)
        out_ref[0, f] = state[f][steps - 1 : steps + depth + 1, own]
    for j in range(1, steps + 1):
        middle = [x[1:-1] for x in state]
        rate = plane_rates([x[:-2] for x in state], middle, [x[2:] for x in state])
        state = [middle[f] + step_time * rate[f] + extended(j, f) for f in range(2)]
        halo = steps - j
        for f in range(2):
            if j < steps:
                inner = state[f][halo - 1 : halo + depth + 1]
                out_ref[j, f] = pltpu.roll(inner, 2 * rows_each - half_rows, 1)[:, :rows_each]
            else:
                end_ref[f] = pltpu.roll(state[f], 2 * rows_each - half_rows, 1)[:, :rows_each]
    if out_ref.shape[0] > steps:
        for f in range(2):
            out_ref[steps, f, 1 : depth + 1] = end_ref[f]
            for p in (0, depth + 1):
                out_ref[steps, f, p] = jnp.zeros_like(end_ref[f, 0])


def result_kernel(
    count, flags_ref, come_ref, inner_offset_ref, inner_mid_ref, edges_offset_ref, edges_mid_ref, out_ref
):
    depth = inner_mid_ref.shape[1] + 2

    def whole(f, p):
        full = jnp.concatenate([come_ref[index_of(r, count), f, p + 1] for r in range(count)], axis=0)
        return jnp.where(flag(flags_ref, end_moved, full), pltpu.roll(full, full.shape[0] - half_rows, 0), full)

    planes = [[whole(f, p) for f in range(2)] for p in range(-1, depth + 1)]
    for p in range(depth):
        here = planes[p + 1]
        rate = plane_rates(planes[p], here, planes[p + 2])
        offset_ref, q = either(p, depth, inner_offset_ref, edges_offset_ref)
        mid_ref, q = either(p, depth, inner_mid_ref, edges_mid_ref)
        for f in range(2):
            end = here[f] + step_time * rate[f] + offset_ref[f, q]
            middle = mid_ref[f, q] + 0.5 * (here[f] + end)
            newest = flag(flags_ref, last, end)
            out_ref[0, 0, f, p] = here[f]
            out_ref[0, 1, f, p] = jnp.where(newest, here[f], middle)
            out_ref[0, 2, f, p] = jnp.where(newest, here[f], end)


def swapped(far, near):
    count = lax.axis_size("space")
    far = lax.ppermute(far, "space", [((i + j) % count, (i + 1 - j) % count) for i in range(1, count, 2) for j in range(2)])
    near = lax.ppermute(near, "space", [(i + j, i + 1 - j) for i in range(0, count, 2) for j in range(2)])
    return far, near


def local(states, first_start):
    count = lax.axis_size("tm")
    me = lax.axis_index("tm")
    blocks = chain_blocks(count)
    slab = states[0]
    _, _, depth, rows, cols = slab.shape
    grid = shape(2, depth, rows, cols)
    edge = shape(2, rows, cols)

    newest = me == count - 1
    flags = jnp.stack([
        lax.axis_index("space") & 1 == 0,
        newest,
        ~newest & (kind_of(me + 1) == 1),
        kind_of(me) == 0,
    ]).astype(jnp.int32)
    flags = jnp.broadcast_to(flags[:, None], (4, 128))

    back_one = [(i, (i - 1) % count) for i in range(count)]
    message = shape(3, 2, rows, cols)
    far, near = call(start_kernel, [message] * 2, flags, slab, first_start)
    far, near = swapped(far, near)
    part, fine0 = call(old_kernel, [shape(2, 2, depth, rows, cols), grid], flags, slab, first_start)
    old_first, old_second = call(sum_kernel, [grid] * 2, flags, part, far, near)
    old_first = lax.ppermute(old_first, "tm", back_one)
    old_second = lax.ppermute(old_second, "tm", back_one)

    fine1, rate0, far, near = call(
        functools.partial(node_kernel, 0), [grid] * 2 + [edge] * 2,
        flags, old_first, fine0, far[2], near[2],
    )
    far, near = swapped(far, near)
    fine2, total, far, near = call(
        functools.partial(node_kernel, 1), [grid] * 2 + [edge] * 2,
        flags, old_second, fine1, far, near, rate0,
    )
    known = (flags, total, fine0, fine1, rate0, fine2)

    def offsets_on(planes, *halo):
        some = shape(2, len(planes), rows, cols)
        send, *rest = call(
            functools.partial(offset_kernel, count, planes),
            [shape(count, 2, len(planes), 2 * rows_each, cols), some, some],
            *known, *halo,
        )
        return lax.all_to_all(send, "tm", 0, 0, tiled=True), rest

    far, near = swapped(far, near)
    inner, inner_rest = offsets_on(range(1, depth - 1))
    edges, edges_rest = offsets_on((0, depth - 1), far, near)

    state = [inner[count - 1], edges[count - 1]]
    ends = []
    for first, steps, kind in blocks:
        if ends:
            way = 1 if kind == 0 else -1
            route = [(index_of(r, count), index_of((r + way) % count, count)) for r in range(count)]
            state = [end, lax.ppermute(end, "tm", route)]
        offsets = [x[first - 1 : first - 1 + steps] for x in (inner, edges)]
        message = shape(2, sum(n for _, n in edge_lists(steps)), 2 * rows_each, cols)
        far, near = call(functools.partial(edge_kernel, kind, steps), [message] * 2, flags, *offsets, *state)
        far, near = swapped(far, near)
        kept = steps + (first + steps == count)
        block, end = call(
            functools.partial(block_kernel, kind, steps),
            [shape(kept, 2, depth + 2, rows_each, cols), shape(2, depth, rows_each, cols)],
            flags, *offsets, *state, far, near,
        )
        ends.append(block)
    back = lax.all_to_all(jnp.concatenate(ends), "tm", 0, 0, tiled=True)
    (result,) = call(
        functools.partial(result_kernel, count), [shape(1, 3, 2, depth, rows, cols)], flags, back, *inner_rest, *edges_rest
    )
    return result


def solution(mesh):
    return jax.shard_map(
        local,
        mesh=mesh,
        in_specs=(P("tm", None, None, "space", None, None), P(None, "space", None, None)),
        out_specs=P("tm", None, None, "space", None, None),
        check_vma=False,
    )
```

```python
import functools

import jax
import jax.numpy as jnp
from jax import lax
from jax.experimental import pallas as pl
from jax.experimental.pallas import tpu as pltpu
from jax.sharding import PartitionSpec as P

step_time = 0.25
half_step = 0.125
diffuse = (0.6, 0.3)
feed_rate = 0.04
kill_rate = 0.06
sweep_weights = ((5.0 / 24.0, 1.0 / 3.0, -1.0 / 24.0), (-1.0 / 24.0, 1.0 / 3.0, 5.0 / 24.0))
old_weights = (
    (step_time * 5.0 / 24.0 - half_step, step_time / 3.0, -step_time / 24.0),
    (-step_time / 24.0, step_time / 3.0 - half_step, step_time * 5.0 / 24.0),
)
new_weights = (
    -0.5 * step_time - step_time / 3.0,
    step_time * 2.0 / 3.0,
    0.5 * step_time - step_time / 3.0,
)
rows_each = 8
block_len = 4
half_rows = 4
vmem_bytes = 16 * 1024 * 1024


def rank_of(index, count):
    return index // 2 if index % 2 == 0 else count - 1 - index // 2


def index_of(rank, count):
    return 2 * rank if rank < count // 2 else 2 * (count - 1 - rank) + 1


def chain_blocks(count):
    blocks, first = [], 1
    while first < count:
        steps = min(block_len, count - first)
        blocks.append((first, steps, len(blocks) % 2))
        first += steps
    return blocks


even, last, offset_moved, end_moved = range(4)


def kind_of(slab):
    return jnp.where(slab > 0, ((slab - 1) // block_len) & 1, 2)


def flag(flags_ref, which, like):
    return jnp.broadcast_to(flags_ref[which : which + 1, :], like.shape) != 0


def call(kernel, out_shapes, *args, result_outside=False, scratch=()):
    size = sum(4 * a.size for a in args) + sum(4 * o.size for o in out_shapes)
    return pl.pallas_call(
        kernel,
        out_shape=tuple(out_shapes),
        in_specs=[pl.BlockSpec(memory_space=pltpu.VMEM)] * len(args),
        out_specs=tuple(pl.BlockSpec(memory_space=pl.ANY if result_outside else pltpu.VMEM) for _ in out_shapes),
        scratch_shapes=list(scratch),
        compiler_params=pltpu.CompilerParams(vmem_limit_bytes=vmem_bytes),
        cost_estimate=pl.CostEstimate(flops=10 * size, bytes_accessed=size, transcendentals=0),
    )(*args)


def shape(*dims):
    return jax.ShapeDtypeStruct(dims, jnp.float32)


def plane_sum(x):
    rows, cols = x.shape[-2], x.shape[-1]
    total = pltpu.roll(x, 1, x.ndim - 2) + pltpu.roll(x, rows - 1, x.ndim - 2)
    total = total + pltpu.roll(x, 1, x.ndim - 1) + pltpu.roll(x, cols - 1, x.ndim - 1)
    return total - 6.0 * x


def reactions(s, c):
    product = s * c * c
    return feed_rate * (1.0 - s) - product, product - (feed_rate + kill_rate) * c


def plane_rates(lo, middle, hi):
    lap = [plane_sum(middle[f]) + lo[f] + hi[f] for f in range(2)]
    react = reactions(*middle)
    return [diffuse[f] * lap[f] + react[f] for f in range(2)]


def put_edges(flags_ref, far_ref, near_ref, at, head, tail):
    here = flag(flags_ref, even, head)
    far_ref[at] = jnp.where(here, head, tail)
    near_ref[at] = jnp.where(here, tail, head)


def below(flags_ref, far, near):
    return jnp.where(flag(flags_ref, even, far), far, near)


def above(flags_ref, far, near):
    return jnp.where(flag(flags_ref, even, far), near, far)


def combined(states_ref, way, f, p):
    w = old_weights[way]
    return sum(w[j] * states_ref[j, f, p] for j in range(3))


def start_kernel(flags_ref, states_ref, first_ref, far_ref, near_ref, start_ref):
    depth = states_ref.shape[2]
    for f in range(2):
        for p in range(depth):
            own = states_ref[2, f, p]
            start_ref[f, p] = jnp.where(flag(flags_ref, last, own), first_ref[f, p], own)
        for way in range(2):
            head, tail = combined(states_ref, way, f, 0), combined(states_ref, way, f, depth - 1)
            put_edges(flags_ref, far_ref, near_ref, (way, f), head, tail)
        put_edges(flags_ref, far_ref, near_ref, (2, f), start_ref[f, 0], start_ref[f, depth - 1])


def old_kernel(states_ref, part_ref):
    depth = states_ref.shape[2]
    for p in range(depth):
        react = [reactions(states_ref[j, 0, p], states_ref[j, 1, p]) for j in range(3)]
        for way in range(2):
            for f in range(2):
                middle = combined(states_ref, way, f, p)
                total = plane_sum(middle)
                if p > 0:
                    total = total + combined(states_ref, way, f, p - 1)
                if p < depth - 1:
                    total = total + combined(states_ref, way, f, p + 1)
                part = diffuse[f] * total
                for j in range(3):
                    part = part + old_weights[way][j] * react[j][f]
                part_ref[way, f, p] = part


def sum_kernel(flags_ref, part_ref, far_ref, near_ref, *out_refs):
    depth = part_ref.shape[2]
    for way, out_ref in enumerate(out_refs):
        for f in range(2):
            for p in range(depth):
                total = part_ref[way, f, p]
                if p == 0:
                    total = total + diffuse[f] * below(flags_ref, far_ref[way, f], near_ref[way, f])
                if p == depth - 1:
                    total = total + diffuse[f] * above(flags_ref, far_ref[way, f], near_ref[way, f])
                out_ref[f, p] = total


def planes_with(flags_ref, x_ref, far_ref, near_ref):
    depth = x_ref.shape[1]

    def plane(p):
        if p < 0:
            return [below(flags_ref, far_ref[f], near_ref[f]) for f in range(2)]
        if p >= depth:
            return [above(flags_ref, far_ref[f], near_ref[f]) for f in range(2)]
        return [x_ref[f, p] for f in range(2)]

    return plane


def node_kernel(way, flags_ref, old_ref, x_ref, far_ref, near_ref, *refs):
    depth = x_ref.shape[1]
    plane = planes_with(flags_ref, x_ref, far_ref, near_ref)
    if way == 0:
        next_ref, keep_ref, next_far_ref, next_near_ref = refs
    else:
        rate_ref, next_ref, keep_ref, next_far_ref, next_near_ref = refs
    for p in range(depth):
        rate = plane_rates(plane(p - 1), plane(p), plane(p + 1))
        for f in range(2):
            next_ref[f, p] = x_ref[f, p] + half_step * rate[f] + old_ref[f, p]
            if way == 0:
                keep_ref[f, p] = rate[f]
            else:
                keep_ref[f, p] = new_weights[0] * rate_ref[f, p] + new_weights[1] * rate[f]
    for f in range(2):
        put_edges(flags_ref, next_far_ref, next_near_ref, f, next_ref[f, 0], next_ref[f, depth - 1])


def offset_kernel(
    count, flags_ref, x_ref, far_ref, near_ref, sum_ref, start_ref, node_ref, rate_ref,
    send_ref, offset_ref, mid_ref,
):
    depth = x_ref.shape[1]
    plane = planes_with(flags_ref, x_ref, far_ref, near_ref)
    for p in range(depth):
        rate = plane_rates(plane(p - 1), plane(p), plane(p + 1))
        for f in range(2):
            offset = sum_ref[f, p] + new_weights[2] * rate[f]
            offset_ref[f, p] = offset
            first = start_ref[f, p] + step_time * rate_ref[f, p] + offset
            offset = jnp.where(flag(flags_ref, last, offset), first, offset)
            moved = pltpu.roll(offset, half_rows, 0), pltpu.roll(offset, rows_each, 0)
            offset = jnp.where(flag(flags_ref, offset_moved, offset), *moved)
            offset = jnp.concatenate([offset, offset[:rows_each]], axis=0)
            for i in range(count):
                r = rank_of(i, count)
                send_ref[i, f, p] = offset[r * rows_each : (r + 2) * rows_each]
            mid_ref[f, p] = node_ref[f, p] - 0.5 * (start_ref[f, p] + x_ref[f, p])


def edge_lists(steps):
    return [(0, steps)] + [(j, steps - j) for j in range(1, steps)]


def joined(kind, own, come):
    return jnp.concatenate([come, own] if kind == 0 else [own, come], axis=-2)


def rows_of(kind, state, offsets_ref):
    def plane(a, f, p):
        if a:
            return offsets_ref[a - 1, f, p]
        return state[0][f, p] if len(state) == 1 else joined(kind, state[0][f, p], state[1][f, p])

    return plane


def tiles_in(steps):
    return sum(2 * n - 1 for _, n in edge_lists(steps))


def edge_kernel(kind, steps, flags_ref, offsets_ref, *refs):
    far_ref, near_ref = refs[-2:]
    depth = offsets_ref.shape[2]
    plane = rows_of(kind, refs[:-2], offsets_ref)
    at = 0
    for a, n in edge_lists(steps):
        for away in range(1, n + 1):
            for f in range(2):
                ends = plane(a, f, away - 1), plane(a, f, depth - away)
                if away == n:
                    ends = [pltpu.roll(x, 2 * rows_each - half_rows, 0)[:rows_each] for x in ends]
                    put_edges(flags_ref, far_ref, near_ref, (f, at), *ends)
                else:
                    put_edges(flags_ref, far_ref, near_ref, (f, at), *[x[:rows_each] for x in ends])
                    put_edges(flags_ref, far_ref, near_ref, (f, at + 1), *[x[rows_each:] for x in ends])
            at += 1 if away == n else 2


def block_kernel(kind, steps, flags_ref, offsets_ref, *refs):
    closing = refs[-1].shape[0] > steps
    far_ref, near_ref, out_ref, end_ref = (*refs[-3:], None) if closing else refs[-4:]
    depth = offsets_ref.shape[2]
    plane = rows_of(kind, refs[: -3 if closing else -4], offsets_ref)
    at = {}
    place = 0
    for a, n in edge_lists(steps):
        at[a] = (place, n)
        place += 2 * n - 1

    def halo(a, f, away, side):
        place, n = at[a]
        first = place + 2 * (away - 1)
        tiles = [side(flags_ref, far_ref[f, t], near_ref[f, t]) for t in range(first, first + 1 + (away < n))]
        if away < n:
            return jnp.concatenate(tiles, axis=0)
        return pltpu.roll(jnp.concatenate(tiles * 2, axis=0), half_rows, 0)

    def extended(a, f):
        planes = [plane(a, f, p) for p in range(depth)]
        if a in at:
            aways = range(1, at[a][1] + 1)
            lo = [halo(a, f, away, below) for away in reversed(aways)]
            hi = [halo(a, f, away, above) for away in aways]
            planes = lo + planes + hi
        return jnp.stack(planes)

    state = [extended(0, f) for f in range(2)]
    for f in range(2):
        own = slice(rows_each, None) if kind == 0 else slice(None, rows_each)
        out_ref[0, f] = state[f][steps - 1 : steps + depth + 1, own]
    for j in range(1, steps + 1):
        middle = [x[1:-1] for x in state]
        rate = plane_rates([x[:-2] for x in state], middle, [x[2:] for x in state])
        state = [middle[f] + step_time * rate[f] + extended(j, f) for f in range(2)]
        around = steps - j
        for f in range(2):
            if j < steps:
                inner = state[f][around - 1 : around + depth + 1]
                out_ref[j, f] = pltpu.roll(inner, 2 * rows_each - half_rows, 1)[:, :rows_each]
                continue
            end = pltpu.roll(state[f], 2 * rows_each - half_rows, 1)[:, :rows_each]
            if closing:
                out_ref[steps, f, 1 : depth + 1] = end
                for p in (0, depth + 1):
                    out_ref[steps, f, p] = jnp.zeros_like(end[0])
            else:
                end_ref[f] = end


def result_kernel(count, flags_ref, come_ref, offset_ref, mid_ref, out_hbm, out_ref, sems):
    depth = mid_ref.shape[1]

    def whole(f, p):
        full = jnp.concatenate([come_ref[index_of(r, count), f, p + 1] for r in range(count)], axis=0)
        return jnp.where(flag(flags_ref, end_moved, full), pltpu.roll(full, full.shape[0] - half_rows, 0), full)

    planes = [[whole(f, p) for f in range(2)] for p in range(-1, depth + 1)]
    copies = []
    for p in range(depth):
        here = planes[p + 1]
        rate = plane_rates(planes[p], here, planes[p + 2])
        for f in range(2):
            end = here[f] + step_time * rate[f] + offset_ref[f, p]
            middle = mid_ref[f, p] + 0.5 * (here[f] + end)
            newest = flag(flags_ref, last, end)
            out_ref[p, 0, f] = here[f]
            out_ref[p, 1, f] = jnp.where(newest, here[f], middle)
            out_ref[p, 2, f] = jnp.where(newest, here[f], end)
        copies.append(pltpu.make_async_copy(out_ref.at[p], out_hbm.at[0, :, :, p], sems.at[p]))
        copies[-1].start()
    for copy in copies:
        copy.wait()


def swapped(far, near):
    count = lax.axis_size("space")
    far = lax.ppermute(far, "space", [((i + j) % count, (i + 1 - j) % count) for i in range(1, count, 2) for j in range(2)])
    near = lax.ppermute(near, "space", [(i + j, i + 1 - j) for i in range(0, count, 2) for j in range(2)])
    return far, near


def local(states, first_start):
    count = lax.axis_size("tm")
    me = lax.axis_index("tm")
    blocks = chain_blocks(count)
    slab = states[0]
    _, _, depth, rows, cols = slab.shape
    grid = shape(2, depth, rows, cols)
    edge = shape(2, rows, cols)

    newest = me == count - 1
    flags = jnp.stack([
        lax.axis_index("space") & 1 == 0,
        newest,
        ~newest & (kind_of(me + 1) == 1),
        kind_of(me) == 0,
    ]).astype(jnp.int32)
    flags = jnp.broadcast_to(flags[:, None], (4, 128))

    back_one = [(i, (i - 1) % count) for i in range(count)]
    message = shape(3, 2, rows, cols)
    far, near, fine0 = call(start_kernel, [message, message, grid], flags, slab, first_start)
    far, near = swapped(far, near)
    (part,) = call(old_kernel, [shape(2, 2, depth, rows, cols)], slab)
    old_first, old_second = call(sum_kernel, [grid] * 2, flags, part, far, near)
    old_first = lax.ppermute(old_first, "tm", back_one)
    old_second = lax.ppermute(old_second, "tm", back_one)

    fine1, rate0, far, near = call(
        functools.partial(node_kernel, 0), [grid] * 2 + [edge] * 2,
        flags, old_first, fine0, far[2], near[2],
    )
    far, near = swapped(far, near)
    fine2, total, far, near = call(
        functools.partial(node_kernel, 1), [grid] * 2 + [edge] * 2,
        flags, old_second, fine1, far, near, rate0,
    )
    far, near = swapped(far, near)
    send, offset, mid = call(
        functools.partial(offset_kernel, count),
        [shape(count, 2, depth, 2 * rows_each, cols), grid, grid],
        flags, fine2, far, near, total, fine0, fine1, rate0,
    )
    held = lax.all_to_all(send, "tm", 0, 0, tiled=True)

    state = [held[count - 1]]
    ends = []
    for first, steps, kind in blocks:
        if ends:
            way = 1 if kind == 0 else -1
            route = [(index_of(r, count), index_of((r + way) % count, count)) for r in range(count)]
            state = [end[0], lax.ppermute(end[0], "tm", route)]
        offsets = held[first - 1 : first - 1 + steps]
        message = shape(2, tiles_in(steps), rows_each, cols)
        far, near = call(functools.partial(edge_kernel, kind, steps), [message] * 2, flags, offsets, *state)
        far, near = swapped(far, near)
        closing = first + steps == count
        block, *end = call(
            functools.partial(block_kernel, kind, steps),
            [shape(steps + closing, 2, depth + 2, rows_each, cols)]
            + [shape(2, depth, rows_each, cols)] * (not closing),
            flags, offsets, *state, far, near,
        )
        ends.append(block)
    back = lax.all_to_all(jnp.concatenate(ends), "tm", 0, 0, tiled=True)
    (result,) = call(
        functools.partial(result_kernel, count), [shape(1, 3, 2, depth, rows, cols)], flags, back, offset, mid,
        result_outside=True,
        scratch=[pltpu.VMEM((depth, 3, 2, rows, cols), jnp.float32), pltpu.SemaphoreType.DMA((depth,))],
    )
    return result


def solution(mesh):
    return jax.shard_map(
        local,
        mesh=mesh,
        in_specs=(P("tm", None, None, "space", None, None), P(None, "space", None, None)),
        out_specs=P("tm", None, None, "space", None, None),
        check_vma=False,
    )
```

```python
import functools

import jax
import jax.numpy as jnp
from jax import lax
from jax.experimental import pallas as pl
from jax.experimental.pallas import tpu as pltpu
from jax.sharding import PartitionSpec as P

step_time = 0.25
half_step = 0.125
diffuse = (0.6, 0.3)
feed_rate = 0.04
kill_rate = 0.06
sweep_weights = ((5.0 / 24.0, 1.0 / 3.0, -1.0 / 24.0), (-1.0 / 24.0, 1.0 / 3.0, 5.0 / 24.0))
old_weights = (
    (step_time * 5.0 / 24.0 - half_step, step_time / 3.0, -step_time / 24.0),
    (-step_time / 24.0, step_time / 3.0 - half_step, step_time * 5.0 / 24.0),
)
new_weights = (
    -0.5 * step_time - step_time / 3.0,
    step_time * 2.0 / 3.0,
    0.5 * step_time - step_time / 3.0,
)
rows_each = 8
block_len = 4
half_rows = 4
rows_sent = 14
vmem_bytes = 16 * 1024 * 1024


def rank_of(index, count):
    return index // 2 if index % 2 == 0 else count - 1 - index // 2


def index_of(rank, count):
    return 2 * rank if rank < count // 2 else 2 * (count - 1 - rank) + 1


def chain_blocks(count):
    ends = [min(b, count) for b in range(block_len, count + block_len, block_len)]
    firsts = [1] + ends[:-1]
    return [(a, b - a, n % 2) for n, (a, b) in enumerate(zip(firsts, ends)) if b > a]


even, last, offset_moved, end_moved = range(4)


def kind_of(slab):
    return (slab // block_len) & 1


def flag(flags_ref, which, like):
    return jnp.broadcast_to(flags_ref[which : which + 1, :], like.shape) != 0


def call(kernel, out_shapes, *args, result_outside=False, scratch=()):
    size = sum(4 * a.size for a in args) + sum(4 * o.size for o in out_shapes)
    return pl.pallas_call(
        kernel,
        out_shape=tuple(out_shapes),
        in_specs=[pl.BlockSpec(memory_space=pltpu.VMEM)] * len(args),
        out_specs=tuple(pl.BlockSpec(memory_space=pl.ANY if result_outside else pltpu.VMEM) for _ in out_shapes),
        scratch_shapes=list(scratch),
        compiler_params=pltpu.CompilerParams(vmem_limit_bytes=vmem_bytes),
        cost_estimate=pl.CostEstimate(flops=10 * size, bytes_accessed=size, transcendentals=0),
    )(*args)


def shape(*dims):
    return jax.ShapeDtypeStruct(dims, jnp.float32)


def plane_sum(x):
    rows, cols = x.shape[-2], x.shape[-1]
    total = pltpu.roll(x, 1, x.ndim - 2) + pltpu.roll(x, rows - 1, x.ndim - 2)
    total = total + pltpu.roll(x, 1, x.ndim - 1) + pltpu.roll(x, cols - 1, x.ndim - 1)
    return total - 6.0 * x


def reactions(s, c):
    product = s * c * c
    return feed_rate * (1.0 - s) - product, product - (feed_rate + kill_rate) * c


def plane_rates(lo, middle, hi):
    lap = [plane_sum(middle[f]) + lo[f] + hi[f] for f in range(2)]
    react = reactions(*middle)
    return [diffuse[f] * lap[f] + react[f] for f in range(2)]


def put_edges(flags_ref, far_ref, near_ref, at, head, tail):
    here = flag(flags_ref, even, head)
    far_ref[at] = jnp.where(here, head, tail)
    near_ref[at] = jnp.where(here, tail, head)


def below(flags_ref, far, near):
    return jnp.where(flag(flags_ref, even, far), far, near)


def above(flags_ref, far, near):
    return jnp.where(flag(flags_ref, even, far), near, far)


def combined(states_ref, way, f, p):
    w = old_weights[way]
    return sum(w[j] * states_ref[j, f, p] for j in range(3))


def start_kernel(flags_ref, states_ref, first_ref, far_ref, near_ref, start_ref):
    depth = states_ref.shape[2]
    for f in range(2):
        for p in range(depth):
            own = states_ref[2, f, p]
            start_ref[f, p] = jnp.where(flag(flags_ref, last, own), first_ref[f, p], own)
        for way in range(2):
            head, tail = combined(states_ref, way, f, 0), combined(states_ref, way, f, depth - 1)
            put_edges(flags_ref, far_ref, near_ref, (way, f), head, tail)
        put_edges(flags_ref, far_ref, near_ref, (2, f), start_ref[f, 0], start_ref[f, depth - 1])


def old_kernel(states_ref, part_ref):
    depth = states_ref.shape[2]
    for p in range(depth):
        react = [reactions(states_ref[j, 0, p], states_ref[j, 1, p]) for j in range(3)]
        for way in range(2):
            for f in range(2):
                middle = combined(states_ref, way, f, p)
                total = plane_sum(middle)
                if p > 0:
                    total = total + combined(states_ref, way, f, p - 1)
                if p < depth - 1:
                    total = total + combined(states_ref, way, f, p + 1)
                part = diffuse[f] * total
                for j in range(3):
                    part = part + old_weights[way][j] * react[j][f]
                part_ref[way, f, p] = part


def sum_kernel(flags_ref, part_ref, far_ref, near_ref, *out_refs):
    depth = part_ref.shape[2]
    for way, out_ref in enumerate(out_refs):
        for f in range(2):
            for p in range(depth):
                total = part_ref[way, f, p]
                if p == 0:
                    total = total + diffuse[f] * below(flags_ref, far_ref[way, f], near_ref[way, f])
                if p == depth - 1:
                    total = total + diffuse[f] * above(flags_ref, far_ref[way, f], near_ref[way, f])
                out_ref[f, p] = total


def planes_with(flags_ref, x_ref, far_ref, near_ref):
    depth = x_ref.shape[1]

    def plane(p):
        if p < 0:
            return [below(flags_ref, far_ref[f], near_ref[f]) for f in range(2)]
        if p >= depth:
            return [above(flags_ref, far_ref[f], near_ref[f]) for f in range(2)]
        return [x_ref[f, p] for f in range(2)]

    return plane


def node_kernel(way, flags_ref, old_ref, x_ref, far_ref, near_ref, *refs):
    depth = x_ref.shape[1]
    plane = planes_with(flags_ref, x_ref, far_ref, near_ref)
    if way == 0:
        next_ref, keep_ref, next_far_ref, next_near_ref = refs
    else:
        rate_ref, next_ref, keep_ref, next_far_ref, next_near_ref = refs
    for p in range(depth):
        rate = plane_rates(plane(p - 1), plane(p), plane(p + 1))
        for f in range(2):
            next_ref[f, p] = x_ref[f, p] + half_step * rate[f] + old_ref[f, p]
            if way == 0:
                keep_ref[f, p] = rate[f]
            else:
                keep_ref[f, p] = new_weights[0] * rate_ref[f, p] + new_weights[1] * rate[f]
    for f in range(2):
        put_edges(flags_ref, next_far_ref, next_near_ref, f, next_ref[f, 0], next_ref[f, depth - 1])


def offset_kernel(
    count, flags_ref, x_ref, far_ref, near_ref, sum_ref, start_ref, node_ref, rate_ref,
    send_ref, offset_ref, mid_ref,
):
    depth = x_ref.shape[1]
    plane = planes_with(flags_ref, x_ref, far_ref, near_ref)
    for p in range(depth):
        rate = plane_rates(plane(p - 1), plane(p), plane(p + 1))
        for f in range(2):
            offset = sum_ref[f, p] + new_weights[2] * rate[f]
            offset_ref[f, p] = offset
            first = start_ref[f, p] + step_time * rate_ref[f, p] + offset
            offset = jnp.where(flag(flags_ref, last, offset), first, offset)
            moved = pltpu.roll(offset, half_rows, 0), pltpu.roll(offset, rows_each, 0)
            offset = jnp.where(flag(flags_ref, offset_moved, offset), *moved)
            offset = jnp.concatenate([offset, offset[: 2 * rows_each]], axis=0)
            place = rows_sent * p
            shift = (place - 1) % rows_each
            if shift:
                offset = pltpu.roll(offset, shift, 0)
            for i in range(count):
                start = rank_of(i, count) * rows_each + 1 + shift
                send_ref[i, f, place : place + rows_sent] = offset[start : start + rows_sent]
            mid_ref[f, p] = node_ref[f, p] - 0.5 * (start_ref[f, p] + x_ref[f, p])


def edge_lists(steps):
    return [(0, steps)] + [(j, steps - j) for j in range(1, steps)]


def joined(kind, own, come):
    return jnp.concatenate([come, own] if kind == 0 else [own, come], axis=-2)


def rows_of(kind, state, offsets_ref):
    kept = 2 * rows_each

    def unpacked(ref, *at):
        p = at[-1]
        total = ref.shape[-2]
        start = min(max(rows_sent * p - 1, 0), total - kept)
        rows = ref[(*at[:-1], slice(start, start + kept))]
        shift = (start + 1 - rows_sent * p) % kept
        return pltpu.roll(rows, shift, 0) if shift else rows

    def plane(a, f, p):
        if a:
            return unpacked(offsets_ref, a - 1, f, p)
        if len(state) == 1:
            return unpacked(state[0], f, p)
        return joined(kind, state[0][f, p], state[1][f, p])

    return plane


def tiles_in(steps):
    return sum(2 * n - 1 for _, n in edge_lists(steps))


def edge_kernel(kind, steps, flags_ref, offsets_ref, *refs):
    far_ref, near_ref = refs[-2:]
    depth = offsets_ref.shape[2] // rows_sent
    plane = rows_of(kind, refs[:-2], offsets_ref)
    at = 0
    for a, n in edge_lists(steps):
        for away in range(1, n + 1):
            for f in range(2):
                ends = plane(a, f, away - 1), plane(a, f, depth - away)
                if away == n:
                    ends = [pltpu.roll(x, 2 * rows_each - half_rows, 0)[:rows_each] for x in ends]
                    put_edges(flags_ref, far_ref, near_ref, (f, at), *ends)
                else:
                    put_edges(flags_ref, far_ref, near_ref, (f, at), *[x[:rows_each] for x in ends])
                    put_edges(flags_ref, far_ref, near_ref, (f, at + 1), *[x[rows_each:] for x in ends])
            at += 1 if away == n else 2


def block_kernel(kind, steps, flags_ref, offsets_ref, *refs):
    closing = refs[-1].shape[0] > steps
    far_ref, near_ref, out_ref, end_ref = (*refs[-3:], None) if closing else refs[-4:]
    depth = offsets_ref.shape[2] // rows_sent
    state = refs[: -3 if closing else -4]
    opening = len(state) == 1
    plane = rows_of(kind, state, offsets_ref)
    at = {}
    place = 0
    for a, n in edge_lists(steps):
        at[a] = (place, n)
        place += 2 * n - 1

    def halo(a, f, away, side):
        place, n = at[a]
        first = place + 2 * (away - 1)
        tiles = [side(flags_ref, far_ref[f, t], near_ref[f, t]) for t in range(first, first + 1 + (away < n))]
        if away < n:
            return jnp.concatenate(tiles, axis=0)
        return pltpu.roll(jnp.concatenate(tiles * 2, axis=0), half_rows, 0)

    def extended(a, f):
        planes = [plane(a, f, p) for p in range(depth)]
        if a in at:
            aways = range(1, at[a][1] + 1)
            lo = [halo(a, f, away, below) for away in reversed(aways)]
            hi = [halo(a, f, away, above) for away in aways]
            planes = lo + planes + hi
        return jnp.stack(planes)

    state = [extended(0, f) for f in range(2)]
    for f in range(2):
        before = state[f][steps - 1 : steps + depth + 1]
        if opening:
            out_ref[0, f] = pltpu.roll(before, 2 * rows_each - half_rows, 1)[:, :rows_each]
        else:
            out_ref[0, f] = before[:, rows_each:] if kind == 0 else before[:, :rows_each]
    for j in range(1, steps + 1):
        middle = [x[1:-1] for x in state]
        rate = plane_rates([x[:-2] for x in state], middle, [x[2:] for x in state])
        state = [middle[f] + step_time * rate[f] + extended(j, f) for f in range(2)]
        around = steps - j
        for f in range(2):
            if j < steps:
                inner = state[f][around - 1 : around + depth + 1]
                out_ref[j, f] = pltpu.roll(inner, 2 * rows_each - half_rows, 1)[:, :rows_each]
                continue
            end = pltpu.roll(state[f], 2 * rows_each - half_rows, 1)[:, :rows_each]
            if closing:
                out_ref[steps, f, 1 : depth + 1] = end
                for p in (0, depth + 1):
                    out_ref[steps, f, p] = jnp.zeros_like(end[0])
            else:
                end_ref[f] = end


def result_kernel(count, flags_ref, come_ref, offset_ref, mid_ref, out_hbm, out_ref, sems):
    depth = mid_ref.shape[1]

    def whole(f, p):
        full = jnp.concatenate([come_ref[index_of(r, count), f, p + 1] for r in range(count)], axis=0)
        return jnp.where(flag(flags_ref, end_moved, full), pltpu.roll(full, full.shape[0] - half_rows, 0), full)

    planes = [[whole(f, p) for f in range(2)] for p in range(-1, depth + 1)]
    copies = []
    for p in range(depth):
        here = planes[p + 1]
        rate = plane_rates(planes[p], here, planes[p + 2])
        for f in range(2):
            end = here[f] + step_time * rate[f] + offset_ref[f, p]
            middle = mid_ref[f, p] + 0.5 * (here[f] + end)
            newest = flag(flags_ref, last, end)
            out_ref[p, 0, f] = here[f]
            out_ref[p, 1, f] = jnp.where(newest, here[f], middle)
            out_ref[p, 2, f] = jnp.where(newest, here[f], end)
        copies.append(pltpu.make_async_copy(out_ref.at[p], out_hbm.at[0, :, :, p], sems.at[p]))
        copies[-1].start()
    for copy in copies:
        copy.wait()


def swapped(far, near):
    count = lax.axis_size("space")
    far = lax.ppermute(far, "space", [((i + j) % count, (i + 1 - j) % count) for i in range(1, count, 2) for j in range(2)])
    near = lax.ppermute(near, "space", [(i + j, i + 1 - j) for i in range(0, count, 2) for j in range(2)])
    return far, near


def local(states, first_start):
    count = lax.axis_size("tm")
    me = lax.axis_index("tm")
    blocks = chain_blocks(count)
    slab = states[0]
    _, _, depth, rows, cols = slab.shape
    grid = shape(2, depth, rows, cols)
    edge = shape(2, rows, cols)

    newest = me == count - 1
    flags = jnp.stack([
        lax.axis_index("space") & 1 == 0,
        newest,
        ~newest & (kind_of(me + 1) == 1),
        kind_of(me) == 0,
    ]).astype(jnp.int32)
    flags = jnp.broadcast_to(flags[:, None], (4, 128))

    back_one = [(i, (i - 1) % count) for i in range(count)]
    message = shape(3, 2, rows, cols)
    far, near, fine0 = call(start_kernel, [message, message, grid], flags, slab, first_start)
    far, near = swapped(far, near)
    (part,) = call(old_kernel, [shape(2, 2, depth, rows, cols)], slab)
    old_first, old_second = call(sum_kernel, [grid] * 2, flags, part, far, near)
    old_first = lax.ppermute(old_first, "tm", back_one)
    old_second = lax.ppermute(old_second, "tm", back_one)

    fine1, rate0, far, near = call(
        functools.partial(node_kernel, 0), [grid] * 2 + [edge] * 2,
        flags, old_first, fine0, far[2], near[2],
    )
    far, near = swapped(far, near)
    fine2, total, far, near = call(
        functools.partial(node_kernel, 1), [grid] * 2 + [edge] * 2,
        flags, old_second, fine1, far, near, rate0,
    )
    far, near = swapped(far, near)
    send, offset, mid = call(
        functools.partial(offset_kernel, count),
        [shape(count, 2, depth * rows_sent, cols), grid, grid],
        flags, fine2, far, near, total, fine0, fine1, rate0,
    )
    held = lax.all_to_all(send, "tm", 0, 0, tiled=True)

    state = [held[count - 1]]
    ends = []
    for first, steps, kind in blocks:
        if ends:
            way = 1 if kind == 0 else -1
            route = [(index_of(r, count), index_of((r + way) % count, count)) for r in range(count)]
            state = [end[0], lax.ppermute(end[0], "tm", route)]
        offsets = held[first - 1 : first - 1 + steps]
        message = shape(2, tiles_in(steps), rows_each, cols)
        far, near = call(functools.partial(edge_kernel, kind, steps), [message] * 2, flags, offsets, *state)
        far, near = swapped(far, near)
        closing = first + steps == count
        block, *end = call(
            functools.partial(block_kernel, kind, steps),
            [shape(steps + closing, 2, depth + 2, rows_each, cols)]
            + [shape(2, depth, rows_each, cols)] * (not closing),
            flags, offsets, *state, far, near,
        )
        ends.append(block)
    back = lax.all_to_all(jnp.concatenate(ends), "tm", 0, 0, tiled=True)
    (result,) = call(
        functools.partial(result_kernel, count), [shape(1, 3, 2, depth, rows, cols)], flags, back, offset, mid,
        result_outside=True,
        scratch=[pltpu.VMEM((depth, 3, 2, rows, cols), jnp.float32), pltpu.SemaphoreType.DMA((depth,))],
    )
    return result


def solution(mesh):
    return jax.shard_map(
        local,
        mesh=mesh,
        in_specs=(P("tm", None, None, "space", None, None), P(None, "space", None, None)),
        out_specs=P("tm", None, None, "space", None, None),
        check_vma=False,
    )
```

```python
import functools

import jax
import jax.numpy as jnp
from jax import lax
from jax.experimental import pallas as pl
from jax.experimental.pallas import tpu as pltpu
from jax.sharding import PartitionSpec as P

step_time = 0.25
half_step = 0.125
diffuse = (0.6, 0.3)
feed_rate = 0.04
kill_rate = 0.06
sweep_weights = ((5.0 / 24.0, 1.0 / 3.0, -1.0 / 24.0), (-1.0 / 24.0, 1.0 / 3.0, 5.0 / 24.0))
old_weights = (
    (step_time * 5.0 / 24.0 - half_step, step_time / 3.0, -step_time / 24.0),
    (-step_time / 24.0, step_time / 3.0 - half_step, step_time * 5.0 / 24.0),
)
new_weights = (
    -0.5 * step_time - step_time / 3.0,
    step_time * 2.0 / 3.0,
    0.5 * step_time - step_time / 3.0,
)
rows_each = 8
block_len = 4
half_rows = 4
rows_sent = 14
vmem_bytes = 16 * 1024 * 1024


def rank_of(index, count):
    return index // 2 if index % 2 == 0 else count - 1 - index // 2


def index_of(rank, count):
    return 2 * rank if rank < count // 2 else 2 * (count - 1 - rank) + 1


def chain_blocks(count):
    ends = [min(b, count) for b in range(block_len, count + block_len, block_len)]
    firsts = [1] + ends[:-1]
    return [(a, b - a, n % 2) for n, (a, b) in enumerate(zip(firsts, ends)) if b > a]


even, last, offset_moved, end_moved = range(4)


def kind_of(slab):
    return (slab // block_len) & 1


def flag(flags_ref, which, like):
    return jnp.broadcast_to(flags_ref[which : which + 1, :], like.shape) != 0


def call(kernel, out_shapes, *args, result_outside=False, scratch=()):
    size = sum(4 * a.size for a in args) + sum(4 * o.size for o in out_shapes)
    return pl.pallas_call(
        kernel,
        out_shape=tuple(out_shapes),
        in_specs=[pl.BlockSpec(memory_space=pltpu.VMEM)] * len(args),
        out_specs=tuple(pl.BlockSpec(memory_space=pl.ANY if result_outside else pltpu.VMEM) for _ in out_shapes),
        scratch_shapes=list(scratch),
        compiler_params=pltpu.CompilerParams(vmem_limit_bytes=vmem_bytes),
        cost_estimate=pl.CostEstimate(flops=10 * size, bytes_accessed=size, transcendentals=0),
    )(*args)


def shape(*dims):
    return jax.ShapeDtypeStruct(dims, jnp.float32)


def plane_sum(x):
    rows, cols = x.shape[-2], x.shape[-1]
    total = pltpu.roll(x, 1, x.ndim - 2) + pltpu.roll(x, rows - 1, x.ndim - 2)
    total = total + pltpu.roll(x, 1, x.ndim - 1) + pltpu.roll(x, cols - 1, x.ndim - 1)
    return total - 6.0 * x


def reactions(s, c):
    product = s * c * c
    return feed_rate * (1.0 - s) - product, product - (feed_rate + kill_rate) * c


def plane_rates(lo, middle, hi):
    lap = [plane_sum(middle[f]) + lo[f] + hi[f] for f in range(2)]
    react = reactions(*middle)
    return [diffuse[f] * lap[f] + react[f] for f in range(2)]


def put_edges(flags_ref, far_ref, near_ref, at, head, tail):
    here = flag(flags_ref, even, head)
    far_ref[at] = jnp.where(here, head, tail)
    near_ref[at] = jnp.where(here, tail, head)


def below(flags_ref, far, near):
    return jnp.where(flag(flags_ref, even, far), far, near)


def above(flags_ref, far, near):
    return jnp.where(flag(flags_ref, even, far), near, far)


def combined(states_ref, way, f, p):
    w = old_weights[way]
    return sum(w[j] * states_ref[j, f, p] for j in range(3))


def start_kernel(flags_ref, states_ref, first_ref, far_ref, near_ref, start_ref):
    depth = states_ref.shape[2]
    for f in range(2):
        for p in range(depth):
            own = states_ref[2, f, p]
            start_ref[f, p] = jnp.where(flag(flags_ref, last, own), first_ref[f, p], own)
        for way in range(2):
            head, tail = combined(states_ref, way, f, 0), combined(states_ref, way, f, depth - 1)
            put_edges(flags_ref, far_ref, near_ref, (way, f), head, tail)
        put_edges(flags_ref, far_ref, near_ref, (2, f), start_ref[f, 0], start_ref[f, depth - 1])


def old_kernel(states_ref, part_ref):
    depth = states_ref.shape[2]
    for p in range(depth):
        react = [reactions(states_ref[j, 0, p], states_ref[j, 1, p]) for j in range(3)]
        for way in range(2):
            for f in range(2):
                middle = combined(states_ref, way, f, p)
                total = plane_sum(middle)
                if p > 0:
                    total = total + combined(states_ref, way, f, p - 1)
                if p < depth - 1:
                    total = total + combined(states_ref, way, f, p + 1)
                part = diffuse[f] * total
                for j in range(3):
                    part = part + old_weights[way][j] * react[j][f]
                part_ref[way, f, p] = part


def sum_kernel(flags_ref, part_ref, far_ref, near_ref, *out_refs):
    depth = part_ref.shape[2]
    for way, out_ref in enumerate(out_refs):
        for f in range(2):
            for p in range(depth):
                total = part_ref[way, f, p]
                if p == 0:
                    total = total + diffuse[f] * below(flags_ref, far_ref[way, f], near_ref[way, f])
                if p == depth - 1:
                    total = total + diffuse[f] * above(flags_ref, far_ref[way, f], near_ref[way, f])
                out_ref[f, p] = total


def planes_with(flags_ref, x_ref, far_ref, near_ref):
    depth = x_ref.shape[1]

    def plane(p):
        if p < 0:
            return [below(flags_ref, far_ref[f], near_ref[f]) for f in range(2)]
        if p >= depth:
            return [above(flags_ref, far_ref[f], near_ref[f]) for f in range(2)]
        return [x_ref[f, p] for f in range(2)]

    return plane


def node_kernel(way, flags_ref, old_ref, x_ref, far_ref, near_ref, *refs):
    depth = x_ref.shape[1]
    plane = planes_with(flags_ref, x_ref, far_ref, near_ref)
    if way == 0:
        next_ref, keep_ref, next_far_ref, next_near_ref = refs
    else:
        rate_ref, next_ref, keep_ref, next_far_ref, next_near_ref = refs
    for p in range(depth):
        rate = plane_rates(plane(p - 1), plane(p), plane(p + 1))
        for f in range(2):
            next_ref[f, p] = x_ref[f, p] + half_step * rate[f] + old_ref[f, p]
            if way == 0:
                keep_ref[f, p] = rate[f]
            else:
                keep_ref[f, p] = new_weights[0] * rate_ref[f, p] + new_weights[1] * rate[f]
    for f in range(2):
        put_edges(flags_ref, next_far_ref, next_near_ref, f, next_ref[f, 0], next_ref[f, depth - 1])


def offset_kernel(
    count, flags_ref, x_ref, far_ref, near_ref, sum_ref, start_ref, node_ref, rate_ref,
    send_ref, offset_ref, mid_ref,
):
    depth = x_ref.shape[1]
    plane = planes_with(flags_ref, x_ref, far_ref, near_ref)
    for p in range(depth):
        rate = plane_rates(plane(p - 1), plane(p), plane(p + 1))
        for f in range(2):
            offset = sum_ref[f, p] + new_weights[2] * rate[f]
            offset_ref[f, p] = offset
            first = start_ref[f, p] + step_time * rate_ref[f, p] + offset
            offset = jnp.where(flag(flags_ref, last, offset), first, offset)
            moved = pltpu.roll(offset, half_rows, 0), pltpu.roll(offset, rows_each, 0)
            offset = jnp.where(flag(flags_ref, offset_moved, offset), *moved)
            offset = jnp.concatenate([offset, offset[: 2 * rows_each]], axis=0)
            place = rows_sent * p
            shift = (place - 1) % rows_each
            if shift:
                offset = pltpu.roll(offset, shift, 0)
            for i in range(count):
                start = rank_of(i, count) * rows_each + 1 + shift
                send_ref[i, f, place : place + rows_sent] = offset[start : start + rows_sent]
            mid_ref[f, p] = node_ref[f, p] - 0.5 * (start_ref[f, p] + x_ref[f, p])


def edge_lists(steps):
    return [(0, steps)] + [(j, steps - j) for j in range(1, steps)]


def joined(kind, own, come):
    return jnp.concatenate([come, own] if kind == 0 else [own, come], axis=-2)


def unpacked(ref, lead, at, first):
    kept = 2 * rows_each
    start = min(max(at - first, 0), ref.shape[-2] - kept)
    rows = ref[(*lead, slice(start, start + kept))]
    shift = (start + first - at) % kept
    return pltpu.roll(rows, shift, 0) if shift else rows


def rows_of(kind, state, offsets_ref):
    def plane(a, f, p):
        if a:
            return unpacked(offsets_ref, (a - 1, f), rows_sent * p, 1)
        if len(state) == 1:
            return unpacked(state[0], (f,), rows_sent * p, 1)
        return joined(kind, state[0][f, p], state[1][f, p])

    return plane


def edge_pieces(steps):
    pieces, at = [], 0
    for a, n in edge_lists(steps):
        for away in range(1, n + 1):
            around = half_rows if a == 0 and away == 1 else n - away
            first, end = half_rows - around, half_rows + rows_each + around
            pieces.append((a, away, at, first, end))
            at += end - first
    return pieces, -(-at // rows_each) * rows_each


def edge_kernel(kind, steps, flags_ref, offsets_ref, *refs):
    far_ref, near_ref = refs[-2:]
    depth = offsets_ref.shape[2] // rows_sent
    plane = rows_of(kind, refs[:-2], offsets_ref)
    pieces, total = edge_pieces(steps)
    used = 0
    for a, away, at, first, end in pieces:
        used = at + end - first
        for f in range(2):
            ends = plane(a, f, away - 1), plane(a, f, depth - away)
            put_edges(flags_ref, far_ref, near_ref, (f, slice(at, used)), *[x[first:end] for x in ends])
    if used < total:
        for f in range(2):
            for ref in (far_ref, near_ref):
                ref[f, used:total] = jnp.zeros((total - used, ref.shape[-1]), jnp.float32)


def block_kernel(kind, steps, flags_ref, offsets_ref, *refs):
    closing = refs[-1].shape[0] > steps
    far_ref, near_ref, out_ref, end_ref = (*refs[-3:], None) if closing else refs[-4:]
    depth = offsets_ref.shape[2] // rows_sent
    state = refs[: -3 if closing else -4]
    opening = len(state) == 1
    plane = rows_of(kind, state, offsets_ref)
    halos = {}
    for a, away, at, first, _ in edge_pieces(steps)[0]:
        halos.setdefault(a, []).append((at, first))

    def halo(f, piece, side):
        return side(flags_ref, *[unpacked(ref, (f,), *piece) for ref in (far_ref, near_ref)])

    def extended(a, f):
        planes = [plane(a, f, p) for p in range(depth)]
        pieces = halos.get(a, [])
        lo = [halo(f, piece, below) for piece in reversed(pieces)]
        hi = [halo(f, piece, above) for piece in pieces]
        return jnp.stack(lo + planes + hi)

    state = [extended(0, f) for f in range(2)]
    for f in range(2):
        before = state[f][steps - 1 : steps + depth + 1]
        if opening:
            out_ref[0, f] = pltpu.roll(before, 2 * rows_each - half_rows, 1)[:, :rows_each]
        else:
            out_ref[0, f] = before[:, rows_each:] if kind == 0 else before[:, :rows_each]
    for j in range(1, steps + 1):
        middle = [x[1:-1] for x in state]
        rate = plane_rates([x[:-2] for x in state], middle, [x[2:] for x in state])
        state = [middle[f] + step_time * rate[f] + extended(j, f) for f in range(2)]
        around = steps - j
        for f in range(2):
            if j < steps:
                inner = state[f][around - 1 : around + depth + 1]
                out_ref[j, f] = pltpu.roll(inner, 2 * rows_each - half_rows, 1)[:, :rows_each]
                continue
            end = pltpu.roll(state[f], 2 * rows_each - half_rows, 1)[:, :rows_each]
            if closing:
                out_ref[steps, f, 1 : depth + 1] = end
                for p in (0, depth + 1):
                    out_ref[steps, f, p] = jnp.zeros_like(end[0])
            else:
                end_ref[f] = end


def result_kernel(count, flags_ref, come_ref, offset_ref, mid_ref, out_hbm, out_ref, sems):
    depth = mid_ref.shape[1]

    def whole(f, p):
        full = jnp.concatenate([come_ref[index_of(r, count), f, p + 1] for r in range(count)], axis=0)
        return jnp.where(flag(flags_ref, end_moved, full), pltpu.roll(full, full.shape[0] - half_rows, 0), full)

    planes = [[whole(f, p) for f in range(2)] for p in range(-1, depth + 1)]
    copies = []
    for p in range(depth):
        here = planes[p + 1]
        rate = plane_rates(planes[p], here, planes[p + 2])
        for f in range(2):
            end = here[f] + step_time * rate[f] + offset_ref[f, p]
            middle = mid_ref[f, p] + 0.5 * (here[f] + end)
            newest = flag(flags_ref, last, end)
            out_ref[p, 0, f] = here[f]
            out_ref[p, 1, f] = jnp.where(newest, here[f], middle)
            out_ref[p, 2, f] = jnp.where(newest, here[f], end)
        copies.append(pltpu.make_async_copy(out_ref.at[p], out_hbm.at[0, :, :, p], sems.at[p]))
        copies[-1].start()
    for copy in copies:
        copy.wait()


def swapped(far, near):
    count = lax.axis_size("space")
    far = lax.ppermute(far, "space", [((i + j) % count, (i + 1 - j) % count) for i in range(1, count, 2) for j in range(2)])
    near = lax.ppermute(near, "space", [(i + j, i + 1 - j) for i in range(0, count, 2) for j in range(2)])
    return far, near


def local(states, first_start):
    count = lax.axis_size("tm")
    me = lax.axis_index("tm")
    blocks = chain_blocks(count)
    slab = states[0]
    _, _, depth, rows, cols = slab.shape
    grid = shape(2, depth, rows, cols)
    edge = shape(2, rows, cols)

    newest = me == count - 1
    flags = jnp.stack([
        lax.axis_index("space") & 1 == 0,
        newest,
        ~newest & (kind_of(me + 1) == 1),
        kind_of(me) == 0,
    ]).astype(jnp.int32)
    flags = jnp.broadcast_to(flags[:, None], (4, 128))

    back_one = [(i, (i - 1) % count) for i in range(count)]
    message = shape(3, 2, rows, cols)
    far, near, fine0 = call(start_kernel, [message, message, grid], flags, slab, first_start)
    far, near = swapped(far, near)
    (part,) = call(old_kernel, [shape(2, 2, depth, rows, cols)], slab)
    old_first, old_second = call(sum_kernel, [grid] * 2, flags, part, far, near)
    old_first = lax.ppermute(old_first, "tm", back_one)
    old_second = lax.ppermute(old_second, "tm", back_one)

    fine1, rate0, far, near = call(
        functools.partial(node_kernel, 0), [grid] * 2 + [edge] * 2,
        flags, old_first, fine0, far[2], near[2],
    )
    far, near = swapped(far, near)
    fine2, total, far, near = call(
        functools.partial(node_kernel, 1), [grid] * 2 + [edge] * 2,
        flags, old_second, fine1, far, near, rate0,
    )
    far, near = swapped(far, near)
    send, offset, mid = call(
        functools.partial(offset_kernel, count),
        [shape(count, 2, depth * rows_sent, cols), grid, grid],
        flags, fine2, far, near, total, fine0, fine1, rate0,
    )
    held = lax.all_to_all(send, "tm", 0, 0, tiled=True)

    state = [held[count - 1]]
    ends = []
    for first, steps, kind in blocks:
        if ends:
            way = 1 if kind == 0 else -1
            route = [(index_of(r, count), index_of((r + way) % count, count)) for r in range(count)]
            state = [end[0], lax.ppermute(end[0], "tm", route)]
        offsets = held[first - 1 : first - 1 + steps]
        message = shape(2, edge_pieces(steps)[1], cols)
        far, near = call(functools.partial(edge_kernel, kind, steps), [message] * 2, flags, offsets, *state)
        far, near = swapped(far, near)
        closing = first + steps == count
        block, *end = call(
            functools.partial(block_kernel, kind, steps),
            [shape(steps + closing, 2, depth + 2, rows_each, cols)]
            + [shape(2, depth, rows_each, cols)] * (not closing),
            flags, offsets, *state, far, near,
        )
        ends.append(block)
    back = lax.all_to_all(jnp.concatenate(ends), "tm", 0, 0, tiled=True)
    (result,) = call(
        functools.partial(result_kernel, count), [shape(1, 3, 2, depth, rows, cols)], flags, back, offset, mid,
        result_outside=True,
        scratch=[pltpu.VMEM((depth, 3, 2, rows, cols), jnp.float32), pltpu.SemaphoreType.DMA((depth,))],
    )
    return result


def solution(mesh):
    return jax.shard_map(
        local,
        mesh=mesh,
        in_specs=(P("tm", None, None, "space", None, None), P(None, "space", None, None)),
        out_specs=P("tm", None, None, "space", None, None),
        check_vma=False,
    )
```

```python
import functools

import jax
import jax.numpy as jnp
from jax import lax
from jax.experimental import pallas as pl
from jax.experimental.pallas import tpu as pltpu
from jax.sharding import PartitionSpec as P

step_time = 0.25
half_step = 0.125
diffuse = (0.6, 0.3)
feed_rate = 0.04
kill_rate = 0.06
sweep_weights = ((5.0 / 24.0, 1.0 / 3.0, -1.0 / 24.0), (-1.0 / 24.0, 1.0 / 3.0, 5.0 / 24.0))
old_weights = (
    (step_time * 5.0 / 24.0 - half_step, step_time / 3.0, -step_time / 24.0),
    (-step_time / 24.0, step_time / 3.0 - half_step, step_time * 5.0 / 24.0),
)
new_weights = (
    -0.5 * step_time - step_time / 3.0,
    step_time * 2.0 / 3.0,
    0.5 * step_time - step_time / 3.0,
)
rows_each = 8
block_len = 4
half_rows = 4
rows_sent = 14
vmem_bytes = 16 * 1024 * 1024


def rank_of(index, count):
    return index // 2 if index % 2 == 0 else count - 1 - index // 2


def index_of(rank, count):
    return 2 * rank if rank < count // 2 else 2 * (count - 1 - rank) + 1


def chain_blocks(count):
    ends = [min(b, count) for b in range(block_len, count + block_len, block_len)]
    firsts = [1] + ends[:-1]
    return [(a, b - a, n % 2) for n, (a, b) in enumerate(zip(firsts, ends)) if b > a]


even, last, offset_moved, end_moved = range(4)


def kind_of(slab):
    return (slab // block_len) & 1


def flag(flags_ref, which, like):
    return jnp.broadcast_to(flags_ref[which : which + 1, :], like.shape) != 0


def call(kernel, out_shapes, *args, result_outside=False, scratch=()):
    size = sum(4 * a.size for a in args) + sum(4 * o.size for o in out_shapes)
    return pl.pallas_call(
        kernel,
        out_shape=tuple(out_shapes),
        in_specs=[pl.BlockSpec(memory_space=pltpu.VMEM)] * len(args),
        out_specs=tuple(pl.BlockSpec(memory_space=pl.ANY if result_outside else pltpu.VMEM) for _ in out_shapes),
        scratch_shapes=list(scratch),
        compiler_params=pltpu.CompilerParams(vmem_limit_bytes=vmem_bytes),
        cost_estimate=pl.CostEstimate(flops=10 * size, bytes_accessed=size, transcendentals=0),
    )(*args)


def shape(*dims):
    return jax.ShapeDtypeStruct(dims, jnp.float32)


def plane_sum(x):
    rows, cols = x.shape[-2], x.shape[-1]
    total = pltpu.roll(x, 1, x.ndim - 2) + pltpu.roll(x, rows - 1, x.ndim - 2)
    total = total + pltpu.roll(x, 1, x.ndim - 1) + pltpu.roll(x, cols - 1, x.ndim - 1)
    return total - 6.0 * x


def reactions(s, c):
    product = s * c * c
    return feed_rate * (1.0 - s) - product, product - (feed_rate + kill_rate) * c


def plane_rates(lo, middle, hi):
    lap = [plane_sum(middle[f]) + lo[f] + hi[f] for f in range(2)]
    react = reactions(*middle)
    return [diffuse[f] * lap[f] + react[f] for f in range(2)]


def put_edges(flags_ref, far_ref, near_ref, at, head, tail):
    here = flag(flags_ref, even, head)
    far_ref[at] = jnp.where(here, head, tail)
    near_ref[at] = jnp.where(here, tail, head)


def below(flags_ref, far, near):
    return jnp.where(flag(flags_ref, even, far), far, near)


def above(flags_ref, far, near):
    return jnp.where(flag(flags_ref, even, far), near, far)


def combined(states_ref, way, f, p):
    w = old_weights[way]
    return sum(w[j] * states_ref[j, f, p] for j in range(3))


def start_kernel(flags_ref, states_ref, first_ref, far_ref, near_ref, start_ref):
    depth = states_ref.shape[2]
    for f in range(2):
        for p in range(depth):
            own = states_ref[2, f, p]
            start_ref[f, p] = jnp.where(flag(flags_ref, last, own), first_ref[f, p], own)
        for way in range(2):
            head, tail = combined(states_ref, way, f, 0), combined(states_ref, way, f, depth - 1)
            put_edges(flags_ref, far_ref, near_ref, (way, f), head, tail)
        put_edges(flags_ref, far_ref, near_ref, (2, f), start_ref[f, 0], start_ref[f, depth - 1])


def old_kernel(states_ref, part_ref):
    depth = states_ref.shape[2]
    for p in range(depth):
        react = [reactions(states_ref[j, 0, p], states_ref[j, 1, p]) for j in range(3)]
        for way in range(2):
            for f in range(2):
                middle = combined(states_ref, way, f, p)
                total = plane_sum(middle)
                if p > 0:
                    total = total + combined(states_ref, way, f, p - 1)
                if p < depth - 1:
                    total = total + combined(states_ref, way, f, p + 1)
                part = diffuse[f] * total
                for j in range(3):
                    part = part + old_weights[way][j] * react[j][f]
                part_ref[way, f, p] = part


def sum_kernel(flags_ref, near_ref, far_ref, part_ref, *out_refs):
    depth = part_ref.shape[2]
    for way, out_ref in enumerate(out_refs):
        for f in range(2):
            for p in range(depth):
                total = part_ref[way, f, p]
                if p == 0:
                    total = total + diffuse[f] * below(flags_ref, far_ref[way, f], near_ref[way, f])
                if p == depth - 1:
                    total = total + diffuse[f] * above(flags_ref, far_ref[way, f], near_ref[way, f])
                out_ref[f, p] = total


def planes_with(flags_ref, x_ref, far_ref, near_ref):
    depth = x_ref.shape[1]

    def plane(p):
        if p < 0:
            return [below(flags_ref, far_ref[f], near_ref[f]) for f in range(2)]
        if p >= depth:
            return [above(flags_ref, far_ref[f], near_ref[f]) for f in range(2)]
        return [x_ref[f, p] for f in range(2)]

    return plane


def node_kernel(way, flags_ref, old_ref, x_ref, far_ref, near_ref, *refs):
    depth = x_ref.shape[1]
    plane = planes_with(flags_ref, x_ref, far_ref, near_ref)
    if way == 0:
        next_ref, keep_ref, next_far_ref, next_near_ref = refs
    else:
        rate_ref, next_ref, keep_ref, next_far_ref, next_near_ref = refs
    for p in range(depth):
        rate = plane_rates(plane(p - 1), plane(p), plane(p + 1))
        for f in range(2):
            next_ref[f, p] = x_ref[f, p] + half_step * rate[f] + old_ref[f, p]
            if way == 0:
                keep_ref[f, p] = rate[f]
            else:
                keep_ref[f, p] = new_weights[0] * rate_ref[f, p] + new_weights[1] * rate[f]
    for f in range(2):
        put_edges(flags_ref, next_far_ref, next_near_ref, f, next_ref[f, 0], next_ref[f, depth - 1])


def offset_kernel(
    count, flags_ref, x_ref, far_ref, near_ref, sum_ref, start_ref, node_ref, rate_ref,
    send_ref, offset_ref, mid_ref,
):
    depth = x_ref.shape[1]
    plane = planes_with(flags_ref, x_ref, far_ref, near_ref)
    for p in range(depth):
        rate = plane_rates(plane(p - 1), plane(p), plane(p + 1))
        for f in range(2):
            offset = sum_ref[f, p] + new_weights[2] * rate[f]
            offset_ref[f, p] = offset
            first = start_ref[f, p] + step_time * rate_ref[f, p] + offset
            offset = jnp.where(flag(flags_ref, last, offset), first, offset)
            moved = pltpu.roll(offset, half_rows, 0), pltpu.roll(offset, rows_each, 0)
            offset = jnp.where(flag(flags_ref, offset_moved, offset), *moved)
            offset = jnp.concatenate([offset, offset[: 2 * rows_each]], axis=0)
            place = rows_sent * p
            shift = (place - 1) % rows_each
            if shift:
                offset = pltpu.roll(offset, shift, 0)
            for i in range(count):
                start = rank_of(i, count) * rows_each + 1 + shift
                send_ref[i, f, place : place + rows_sent] = offset[start : start + rows_sent]
            mid_ref[f, p] = node_ref[f, p] - 0.5 * (start_ref[f, p] + x_ref[f, p])


def edge_lists(steps):
    return [(0, steps)] + [(j, steps - j) for j in range(1, steps)]


def joined(kind, own, come):
    return jnp.concatenate([come, own] if kind == 0 else [own, come], axis=-2)


def unpacked(ref, lead, at, first):
    kept = 2 * rows_each
    start = min(max(at - first, 0), ref.shape[-2] - kept)
    rows = ref[(*lead, slice(start, start + kept))]
    shift = (start + first - at) % kept
    return pltpu.roll(rows, shift, 0) if shift else rows


def rows_of(kind, state, offsets_ref):
    def plane(a, f, p):
        if a:
            return unpacked(offsets_ref, (a - 1, f), rows_sent * p, 1)
        if len(state) == 1:
            return unpacked(state[0], (f,), rows_sent * p, 1)
        return joined(kind, state[0][f, p], state[1][f, p])

    return plane


def edge_pieces(steps):
    pieces, at = [], 0
    for a, n in edge_lists(steps):
        for away in range(1, n + 1):
            around = half_rows if a == 0 and away == 1 else n - away
            first, end = half_rows - around, half_rows + rows_each + around
            pieces.append((a, away, at, first, end))
            at += end - first
    return pieces, -(-at // rows_each) * rows_each


def edge_kernel(kind, steps, flags_ref, offsets_ref, *refs):
    far_ref, near_ref = refs[-2:]
    depth = offsets_ref.shape[2] // rows_sent
    plane = rows_of(kind, refs[:-2], offsets_ref)
    pieces, total = edge_pieces(steps)
    used = 0
    for a, away, at, first, end in pieces:
        used = at + end - first
        for f in range(2):
            ends = plane(a, f, away - 1), plane(a, f, depth - away)
            put_edges(flags_ref, far_ref, near_ref, (f, slice(at, used)), *[x[first:end] for x in ends])
    if used < total:
        for f in range(2):
            for ref in (far_ref, near_ref):
                ref[f, used:total] = jnp.zeros((total - used, ref.shape[-1]), jnp.float32)


def block_kernel(kind, steps, flags_ref, offsets_ref, *refs):
    closing = refs[-1].shape[0] > steps
    far_ref, near_ref, out_ref, end_ref = (*refs[-3:], None) if closing else refs[-4:]
    depth = offsets_ref.shape[2] // rows_sent
    state = refs[: -3 if closing else -4]
    opening = len(state) == 1
    plane = rows_of(kind, state, offsets_ref)
    halos = {}
    for a, away, at, first, _ in edge_pieces(steps)[0]:
        halos.setdefault(a, []).append((at, first))

    def halo(f, piece, side):
        return side(flags_ref, *[unpacked(ref, (f,), *piece) for ref in (far_ref, near_ref)])

    def extended(a, f):
        planes = [plane(a, f, p) for p in range(depth)]
        pieces = halos.get(a, [])
        lo = [halo(f, piece, below) for piece in reversed(pieces)]
        hi = [halo(f, piece, above) for piece in pieces]
        return jnp.stack(lo + planes + hi)

    state = [extended(0, f) for f in range(2)]
    for f in range(2):
        before = state[f][steps - 1 : steps + depth + 1]
        if opening:
            out_ref[0, f] = pltpu.roll(before, 2 * rows_each - half_rows, 1)[:, :rows_each]
        else:
            out_ref[0, f] = before[:, rows_each:] if kind == 0 else before[:, :rows_each]
    for j in range(1, steps + 1):
        middle = [x[1:-1] for x in state]
        rate = plane_rates([x[:-2] for x in state], middle, [x[2:] for x in state])
        state = [middle[f] + step_time * rate[f] + extended(j, f) for f in range(2)]
        around = steps - j
        for f in range(2):
            if j < steps:
                inner = state[f][around - 1 : around + depth + 1]
                out_ref[j, f] = pltpu.roll(inner, 2 * rows_each - half_rows, 1)[:, :rows_each]
                continue
            end = pltpu.roll(state[f], 2 * rows_each - half_rows, 1)[:, :rows_each]
            if closing:
                out_ref[steps, f, 1 : depth + 1] = end
                for p in (0, depth + 1):
                    out_ref[steps, f, p] = jnp.zeros_like(end[0])
            else:
                end_ref[f] = end


def result_kernel(count, flags_ref, come_ref, offset_ref, mid_ref, out_hbm, out_ref, sems):
    depth = mid_ref.shape[1]

    def whole(f, p):
        full = jnp.concatenate([come_ref[index_of(r, count), f, p + 1] for r in range(count)], axis=0)
        return jnp.where(flag(flags_ref, end_moved, full), pltpu.roll(full, full.shape[0] - half_rows, 0), full)

    planes = [[whole(f, p) for f in range(2)] for p in range(-1, depth + 1)]
    copies = []
    for p in range(depth):
        here = planes[p + 1]
        rate = plane_rates(planes[p], here, planes[p + 2])
        for f in range(2):
            end = here[f] + step_time * rate[f] + offset_ref[f, p]
            middle = mid_ref[f, p] + 0.5 * (here[f] + end)
            newest = flag(flags_ref, last, end)
            out_ref[p, 0, f] = here[f]
            out_ref[p, 1, f] = jnp.where(newest, here[f], middle)
            out_ref[p, 2, f] = jnp.where(newest, here[f], end)
        copies.append(pltpu.make_async_copy(out_ref.at[p], out_hbm.at[0, :, :, p], sems.at[p]))
        copies[-1].start()
    for copy in copies:
        copy.wait()


def swapped(far, near):
    count = lax.axis_size("space")
    far = lax.ppermute(far, "space", [((i + j) % count, (i + 1 - j) % count) for i in range(1, count, 2) for j in range(2)])
    near = lax.ppermute(near, "space", [(i + j, i + 1 - j) for i in range(0, count, 2) for j in range(2)])
    return far, near


def local(states, first_start):
    count = lax.axis_size("tm")
    me = lax.axis_index("tm")
    blocks = chain_blocks(count)
    slab = states[0]
    _, _, depth, rows, cols = slab.shape
    grid = shape(2, depth, rows, cols)
    edge = shape(2, rows, cols)

    newest = me == count - 1
    flags = jnp.stack([
        lax.axis_index("space") & 1 == 0,
        newest,
        ~newest & (kind_of(me + 1) == 1),
        kind_of(me) == 0,
    ]).astype(jnp.int32)
    flags = jnp.broadcast_to(flags[:, None], (4, 128))

    back_one = [(i, (i - 1) % count) for i in range(count)]
    message = shape(3, 2, rows, cols)
    far, near, fine0 = call(start_kernel, [message, message, grid], flags, slab, first_start)
    far, near = swapped(far, near)
    (part,) = call(old_kernel, [shape(2, 2, depth, rows, cols)], slab)
    old_first, old_second = call(sum_kernel, [grid] * 2, flags, near, far, part)
    old_first = lax.ppermute(old_first, "tm", back_one)
    old_second = lax.ppermute(old_second, "tm", back_one)

    fine1, rate0, far, near = call(
        functools.partial(node_kernel, 0), [grid] * 2 + [edge] * 2,
        flags, old_first, fine0, far[2], near[2],
    )
    far, near = swapped(far, near)
    fine2, total, far, near = call(
        functools.partial(node_kernel, 1), [grid] * 2 + [edge] * 2,
        flags, old_second, fine1, far, near, rate0,
    )
    far, near = swapped(far, near)
    send, offset, mid = call(
        functools.partial(offset_kernel, count),
        [shape(count, 2, depth * rows_sent, cols), grid, grid],
        flags, fine2, far, near, total, fine0, fine1, rate0,
    )
    held = lax.all_to_all(send, "tm", 0, 0, tiled=True)

    state = [held[count - 1]]
    ends = []
    for first, steps, kind in blocks:
        if ends:
            way = 1 if kind == 0 else -1
            route = [(index_of(r, count), index_of((r + way) % count, count)) for r in range(count)]
            state = [end[0], lax.ppermute(end[0], "tm", route)]
        offsets = held[first - 1 : first - 1 + steps]
        message = shape(2, edge_pieces(steps)[1], cols)
        far, near = call(functools.partial(edge_kernel, kind, steps), [message] * 2, flags, offsets, *state)
        far, near = swapped(far, near)
        closing = first + steps == count
        block, *end = call(
            functools.partial(block_kernel, kind, steps),
            [shape(steps + closing, 2, depth + 2, rows_each, cols)]
            + [shape(2, depth, rows_each, cols)] * (not closing),
            flags, offsets, *state, far, near,
        )
        ends.append(block)
    back = lax.all_to_all(jnp.concatenate(ends), "tm", 0, 0, tiled=True)
    (result,) = call(
        functools.partial(result_kernel, count), [shape(1, 3, 2, depth, rows, cols)], flags, back, offset, mid,
        result_outside=True,
        scratch=[pltpu.VMEM((depth, 3, 2, rows, cols), jnp.float32), pltpu.SemaphoreType.DMA((depth,))],
    )
    return result


def solution(mesh):
    return jax.shard_map(
        local,
        mesh=mesh,
        in_specs=(P("tm", None, None, "space", None, None), P(None, "space", None, None)),
        out_specs=P("tm", None, None, "space", None, None),
        check_vma=False,
    )
```

```python
import functools

import jax
import jax.numpy as jnp
from jax import lax
from jax.experimental import pallas as pl
from jax.experimental.pallas import tpu as pltpu
from jax.sharding import PartitionSpec as P

step_time = 0.25
half_step = 0.125
diffuse = (0.6, 0.3)
feed_rate = 0.04
kill_rate = 0.06
sweep_weights = ((5.0 / 24.0, 1.0 / 3.0, -1.0 / 24.0), (-1.0 / 24.0, 1.0 / 3.0, 5.0 / 24.0))
old_weights = (
    (step_time * 5.0 / 24.0 - half_step, step_time / 3.0, -step_time / 24.0),
    (-step_time / 24.0, step_time / 3.0 - half_step, step_time * 5.0 / 24.0),
)
new_weights = (
    -0.5 * step_time - step_time / 3.0,
    step_time * 2.0 / 3.0,
    0.5 * step_time - step_time / 3.0,
)
rows_each = 8
block_len = 4
half_rows = 4
rows_sent = 14
vmem_bytes = 16 * 1024 * 1024


def rank_of(index, count):
    return index // 2 if index % 2 == 0 else count - 1 - index // 2


def index_of(rank, count):
    return 2 * rank if rank < count // 2 else 2 * (count - 1 - rank) + 1


def chain_blocks(count):
    ends = [min(b, count) for b in range(block_len, count + block_len, block_len)]
    firsts = [1] + ends[:-1]
    return [(a, b - a, n % 2) for n, (a, b) in enumerate(zip(firsts, ends)) if b > a]


even, last, offset_moved, end_moved = range(4)


def kind_of(slab):
    return (slab // block_len) & 1


def flag(flags_ref, which, like):
    return jnp.broadcast_to(flags_ref[which : which + 1, :], like.shape) != 0


def call(kernel, out_shapes, *args, result_outside=False, scratch=()):
    size = sum(4 * a.size for a in args) + sum(4 * o.size for o in out_shapes)
    return pl.pallas_call(
        kernel,
        out_shape=tuple(out_shapes),
        in_specs=[pl.BlockSpec(memory_space=pltpu.VMEM)] * len(args),
        out_specs=tuple(pl.BlockSpec(memory_space=pl.ANY if result_outside else pltpu.VMEM) for _ in out_shapes),
        scratch_shapes=list(scratch),
        compiler_params=pltpu.CompilerParams(vmem_limit_bytes=vmem_bytes),
        cost_estimate=pl.CostEstimate(flops=10 * size, bytes_accessed=size, transcendentals=0),
    )(*args)


def shape(*dims):
    return jax.ShapeDtypeStruct(dims, jnp.float32)


def plane_sum(x):
    rows, cols = x.shape[-2], x.shape[-1]
    total = pltpu.roll(x, 1, x.ndim - 2) + pltpu.roll(x, rows - 1, x.ndim - 2)
    total = total + pltpu.roll(x, 1, x.ndim - 1) + pltpu.roll(x, cols - 1, x.ndim - 1)
    return total - 6.0 * x


def reactions(s, c):
    product = s * c * c
    return feed_rate * (1.0 - s) - product, product - (feed_rate + kill_rate) * c


def plane_rates(lo, middle, hi):
    lap = [plane_sum(middle[f]) + lo[f] + hi[f] for f in range(2)]
    react = reactions(*middle)
    return [diffuse[f] * lap[f] + react[f] for f in range(2)]


def put_edges(flags_ref, far_ref, near_ref, at, head, tail):
    here = flag(flags_ref, even, head)
    far_ref[at] = jnp.where(here, head, tail)
    near_ref[at] = jnp.where(here, tail, head)


def below(flags_ref, far, near):
    return jnp.where(flag(flags_ref, even, far), far, near)


def above(flags_ref, far, near):
    return jnp.where(flag(flags_ref, even, far), near, far)


def combined(states_ref, way, f, p):
    w = old_weights[way]
    return sum(w[j] * states_ref[j, f, p] for j in range(3))


def start_kernel(flags_ref, states_ref, first_ref, far_ref, near_ref, start_ref):
    depth = states_ref.shape[2]
    for f in range(2):
        for p in range(depth):
            own = states_ref[2, f, p]
            start_ref[f, p] = jnp.where(flag(flags_ref, last, own), first_ref[f, p], own)
        for way in range(2):
            head, tail = combined(states_ref, way, f, 0), combined(states_ref, way, f, depth - 1)
            put_edges(flags_ref, far_ref, near_ref, (way, f), head, tail)
        put_edges(flags_ref, far_ref, near_ref, (2, f), start_ref[f, 0], start_ref[f, depth - 1])


def old_kernel(states_ref, inner_ref, part_ref):
    depth = states_ref.shape[2]
    for p in range(depth):
        react = [reactions(states_ref[j, 0, p], states_ref[j, 1, p]) for j in range(3)]
        for way in range(2):
            for f in range(2):
                middle = combined(states_ref, way, f, p)
                total = plane_sum(middle)
                if p > 0:
                    total = total + combined(states_ref, way, f, p - 1)
                if p < depth - 1:
                    total = total + combined(states_ref, way, f, p + 1)
                part = diffuse[f] * total
                for j in range(3):
                    part = part + old_weights[way][j] * react[j][f]
                if way == 0 and 0 < p < depth - 1:
                    inner_ref[f, p - 1] = part
                else:
                    part_ref[way, f, p] = part


def sum_kernel(flags_ref, part_ref, far_ref, near_ref, edge_ref, second_ref):
    depth = part_ref.shape[2]
    for f in range(2):
        for way in range(2):
            lo = diffuse[f] * below(flags_ref, far_ref[way, f], near_ref[way, f])
            hi = diffuse[f] * above(flags_ref, far_ref[way, f], near_ref[way, f])
            head, tail = part_ref[way, f, 0] + lo, part_ref[way, f, depth - 1] + hi
            if way == 0:
                edge_ref[f, 0] = head
                edge_ref[f, 1] = tail
            else:
                second_ref[f, 0] = head
                second_ref[f, depth - 1] = tail
                for p in range(1, depth - 1):
                    second_ref[f, p] = part_ref[way, f, p]


def planes_with(flags_ref, x_ref, far_ref, near_ref):
    depth = x_ref.shape[1]

    def plane(p):
        if p < 0:
            return [below(flags_ref, far_ref[f], near_ref[f]) for f in range(2)]
        if p >= depth:
            return [above(flags_ref, far_ref[f], near_ref[f]) for f in range(2)]
        return [x_ref[f, p] for f in range(2)]

    return plane


def node_kernel(way, flags_ref, old_ref, x_ref, far_ref, near_ref, *refs):
    depth = x_ref.shape[1]
    plane = planes_with(flags_ref, x_ref, far_ref, near_ref)
    if way == 0:
        edge_ref, next_ref, keep_ref, next_far_ref, next_near_ref = refs
    else:
        rate_ref, next_ref, keep_ref, next_far_ref, next_near_ref = refs
    for p in range(depth):
        rate = plane_rates(plane(p - 1), plane(p), plane(p + 1))
        for f in range(2):
            if way == 1:
                old = old_ref[f, p]
            elif 0 < p < depth - 1:
                old = old_ref[f, p - 1]
            else:
                old = edge_ref[f, min(p, 1)]
            next_ref[f, p] = x_ref[f, p] + half_step * rate[f] + old
            if way == 0:
                keep_ref[f, p] = rate[f]
            else:
                keep_ref[f, p] = new_weights[0] * rate_ref[f, p] + new_weights[1] * rate[f]
    for f in range(2):
        put_edges(flags_ref, next_far_ref, next_near_ref, f, next_ref[f, 0], next_ref[f, depth - 1])


def offset_kernel(
    count, flags_ref, x_ref, far_ref, near_ref, sum_ref, start_ref, node_ref, rate_ref,
    send_ref, offset_ref, mid_ref,
):
    depth = x_ref.shape[1]
    plane = planes_with(flags_ref, x_ref, far_ref, near_ref)
    for p in range(depth):
        rate = plane_rates(plane(p - 1), plane(p), plane(p + 1))
        for f in range(2):
            offset = sum_ref[f, p] + new_weights[2] * rate[f]
            offset_ref[f, p] = offset
            first = start_ref[f, p] + step_time * rate_ref[f, p] + offset
            offset = jnp.where(flag(flags_ref, last, offset), first, offset)
            moved = pltpu.roll(offset, half_rows, 0), pltpu.roll(offset, rows_each, 0)
            offset = jnp.where(flag(flags_ref, offset_moved, offset), *moved)
            offset = jnp.concatenate([offset, offset[: 2 * rows_each]], axis=0)
            place = rows_sent * p
            shift = (place - 1) % rows_each
            if shift:
                offset = pltpu.roll(offset, shift, 0)
            for i in range(count):
                start = rank_of(i, count) * rows_each + 1 + shift
                send_ref[i, f, place : place + rows_sent] = offset[start : start + rows_sent]
            mid_ref[f, p] = node_ref[f, p] - 0.5 * (start_ref[f, p] + x_ref[f, p])


def edge_lists(steps):
    return [(0, steps)] + [(j, steps - j) for j in range(1, steps)]


def joined(kind, own, come):
    return jnp.concatenate([come, own] if kind == 0 else [own, come], axis=-2)


def unpacked(ref, lead, at, first):
    kept = 2 * rows_each
    start = min(max(at - first, 0), ref.shape[-2] - kept)
    rows = ref[(*lead, slice(start, start + kept))]
    shift = (start + first - at) % kept
    return pltpu.roll(rows, shift, 0) if shift else rows


def rows_of(kind, state, offsets_ref):
    def plane(a, f, p):
        if a:
            return unpacked(offsets_ref, (a - 1, f), rows_sent * p, 1)
        if len(state) == 1:
            return unpacked(state[0], (f,), rows_sent * p, 1)
        return joined(kind, state[0][f, p], state[1][f, p])

    return plane


def edge_pieces(steps):
    pieces, at = [], 0
    for a, n in edge_lists(steps):
        for away in range(1, n + 1):
            around = half_rows if a == 0 and away == 1 else n - away
            first, end = half_rows - around, half_rows + rows_each + around
            pieces.append((a, away, at, first, end))
            at += end - first
    return pieces, -(-at // rows_each) * rows_each


def edge_kernel(kind, steps, flags_ref, offsets_ref, *refs):
    far_ref, near_ref = refs[-2:]
    depth = offsets_ref.shape[2] // rows_sent
    plane = rows_of(kind, refs[:-2], offsets_ref)
    pieces, total = edge_pieces(steps)
    used = 0
    for a, away, at, first, end in pieces:
        used = at + end - first
        for f in range(2):
            ends = plane(a, f, away - 1), plane(a, f, depth - away)
            put_edges(flags_ref, far_ref, near_ref, (f, slice(at, used)), *[x[first:end] for x in ends])
    if used < total:
        for f in range(2):
            for ref in (far_ref, near_ref):
                ref[f, used:total] = jnp.zeros((total - used, ref.shape[-1]), jnp.float32)


def block_kernel(kind, steps, flags_ref, offsets_ref, *refs):
    closing = refs[-1].shape[0] > steps
    far_ref, near_ref, out_ref, end_ref = (*refs[-3:], None) if closing else refs[-4:]
    depth = offsets_ref.shape[2] // rows_sent
    state = refs[: -3 if closing else -4]
    opening = len(state) == 1
    plane = rows_of(kind, state, offsets_ref)
    halos = {}
    for a, away, at, first, _ in edge_pieces(steps)[0]:
        halos.setdefault(a, []).append((at, first))

    def halo(f, piece, side):
        return side(flags_ref, *[unpacked(ref, (f,), *piece) for ref in (far_ref, near_ref)])

    def extended(a, f):
        planes = [plane(a, f, p) for p in range(depth)]
        pieces = halos.get(a, [])
        lo = [halo(f, piece, below) for piece in reversed(pieces)]
        hi = [halo(f, piece, above) for piece in pieces]
        return jnp.stack(lo + planes + hi)

    state = [extended(0, f) for f in range(2)]
    for f in range(2):
        before = state[f][steps - 1 : steps + depth + 1]
        if opening:
            out_ref[0, f] = pltpu.roll(before, 2 * rows_each - half_rows, 1)[:, :rows_each]
        else:
            out_ref[0, f] = before[:, rows_each:] if kind == 0 else before[:, :rows_each]
    for j in range(1, steps + 1):
        middle = [x[1:-1] for x in state]
        rate = plane_rates([x[:-2] for x in state], middle, [x[2:] for x in state])
        state = [middle[f] + step_time * rate[f] + extended(j, f) for f in range(2)]
        around = steps - j
        for f in range(2):
            if j < steps:
                inner = state[f][around - 1 : around + depth + 1]
                out_ref[j, f] = pltpu.roll(inner, 2 * rows_each - half_rows, 1)[:, :rows_each]
                continue
            end = pltpu.roll(state[f], 2 * rows_each - half_rows, 1)[:, :rows_each]
            if closing:
                out_ref[steps, f, 1 : depth + 1] = end
                for p in (0, depth + 1):
                    out_ref[steps, f, p] = jnp.zeros_like(end[0])
            else:
                end_ref[f] = end


def result_kernel(count, flags_ref, come_ref, offset_ref, mid_ref, out_hbm, out_ref, sems):
    depth = mid_ref.shape[1]

    def whole(f, p):
        full = jnp.concatenate([come_ref[index_of(r, count), f, p + 1] for r in range(count)], axis=0)
        return jnp.where(flag(flags_ref, end_moved, full), pltpu.roll(full, full.shape[0] - half_rows, 0), full)

    planes = [[whole(f, p) for f in range(2)] for p in range(-1, depth + 1)]
    copies = []
    for p in range(depth):
        here = planes[p + 1]
        rate = plane_rates(planes[p], here, planes[p + 2])
        for f in range(2):
            end = here[f] + step_time * rate[f] + offset_ref[f, p]
            middle = mid_ref[f, p] + 0.5 * (here[f] + end)
            newest = flag(flags_ref, last, end)
            out_ref[p, 0, f] = here[f]
            out_ref[p, 1, f] = jnp.where(newest, here[f], middle)
            out_ref[p, 2, f] = jnp.where(newest, here[f], end)
        copies.append(pltpu.make_async_copy(out_ref.at[p], out_hbm.at[0, :, :, p], sems.at[p]))
        copies[-1].start()
    for copy in copies:
        copy.wait()


def swapped(far, near):
    count = lax.axis_size("space")
    far = lax.ppermute(far, "space", [((i + j) % count, (i + 1 - j) % count) for i in range(1, count, 2) for j in range(2)])
    near = lax.ppermute(near, "space", [(i + j, i + 1 - j) for i in range(0, count, 2) for j in range(2)])
    return far, near


def local(states, first_start):
    count = lax.axis_size("tm")
    me = lax.axis_index("tm")
    blocks = chain_blocks(count)
    slab = states[0]
    _, _, depth, rows, cols = slab.shape
    grid = shape(2, depth, rows, cols)
    edge = shape(2, rows, cols)

    newest = me == count - 1
    flags = jnp.stack([
        lax.axis_index("space") & 1 == 0,
        newest,
        ~newest & (kind_of(me + 1) == 1),
        kind_of(me) == 0,
    ]).astype(jnp.int32)
    flags = jnp.broadcast_to(flags[:, None], (4, 128))

    back_one = [(i, (i - 1) % count) for i in range(count)]
    message = shape(3, 2, rows, cols)
    far, near, fine0 = call(start_kernel, [message, message, grid], flags, slab, first_start)
    far, near = swapped(far, near)
    inner, part = call(
        old_kernel, [shape(2, depth - 2, rows, cols), shape(2, 2, depth, rows, cols)], slab
    )
    inner = lax.ppermute(inner, "tm", back_one)
    edges, old_second = call(sum_kernel, [shape(2, 2, rows, cols), grid], flags, part, far, near)
    edges = lax.ppermute(edges, "tm", back_one)
    old_second = lax.ppermute(old_second, "tm", back_one)

    fine1, rate0, far, near = call(
        functools.partial(node_kernel, 0), [grid] * 2 + [edge] * 2,
        flags, inner, fine0, far[2], near[2], edges,
    )
    far, near = swapped(far, near)
    fine2, total, far, near = call(
        functools.partial(node_kernel, 1), [grid] * 2 + [edge] * 2,
        flags, old_second, fine1, far, near, rate0,
    )
    far, near = swapped(far, near)
    send, offset, mid = call(
        functools.partial(offset_kernel, count),
        [shape(count, 2, depth * rows_sent, cols), grid, grid],
        flags, fine2, far, near, total, fine0, fine1, rate0,
    )
    held = lax.all_to_all(send, "tm", 0, 0, tiled=True)

    state = [held[count - 1]]
    ends = []
    for first, steps, kind in blocks:
        if ends:
            way = 1 if kind == 0 else -1
            route = [(index_of(r, count), index_of((r + way) % count, count)) for r in range(count)]
            state = [end[0], lax.ppermute(end[0], "tm", route)]
        offsets = held[first - 1 : first - 1 + steps]
        message = shape(2, edge_pieces(steps)[1], cols)
        far, near = call(functools.partial(edge_kernel, kind, steps), [message] * 2, flags, offsets, *state)
        far, near = swapped(far, near)
        closing = first + steps == count
        block, *end = call(
            functools.partial(block_kernel, kind, steps),
            [shape(steps + closing, 2, depth + 2, rows_each, cols)]
            + [shape(2, depth, rows_each, cols)] * (not closing),
            flags, offsets, *state, far, near,
        )
        ends.append(block)
    back = lax.all_to_all(jnp.concatenate(ends), "tm", 0, 0, tiled=True)
    (result,) = call(
        functools.partial(result_kernel, count), [shape(1, 3, 2, depth, rows, cols)], flags, back, offset, mid,
        result_outside=True,
        scratch=[pltpu.VMEM((depth, 3, 2, rows, cols), jnp.float32), pltpu.SemaphoreType.DMA((depth,))],
    )
    return result


def solution(mesh):
    return jax.shard_map(
        local,
        mesh=mesh,
        in_specs=(P("tm", None, None, "space", None, None), P(None, "space", None, None)),
        out_specs=P("tm", None, None, "space", None, None),
        check_vma=False,
    )
```

```python
import functools

import jax
import jax.numpy as jnp
from jax import lax
from jax.experimental import pallas as pl
from jax.experimental.pallas import tpu as pltpu
from jax.sharding import PartitionSpec as P

step_time = 0.25
half_step = 0.125
diffuse = (0.6, 0.3)
feed_rate = 0.04
kill_rate = 0.06
sweep_weights = ((5.0 / 24.0, 1.0 / 3.0, -1.0 / 24.0), (-1.0 / 24.0, 1.0 / 3.0, 5.0 / 24.0))
old_weights = (
    (step_time * 5.0 / 24.0 - half_step, step_time / 3.0, -step_time / 24.0),
    (-step_time / 24.0, step_time / 3.0 - half_step, step_time * 5.0 / 24.0),
)
new_weights = (
    -0.5 * step_time - step_time / 3.0,
    step_time * 2.0 / 3.0,
    0.5 * step_time - step_time / 3.0,
)
rows_each = 8
block_len = 4
half_rows = 4
rows_sent = 14
vmem_bytes = 16 * 1024 * 1024


def rank_of(index, count):
    return index // 2 if index % 2 == 0 else count - 1 - index // 2


def index_of(rank, count):
    return 2 * rank if rank < count // 2 else 2 * (count - 1 - rank) + 1


def chain_blocks(count):
    ends = [min(b, count) for b in range(block_len, count + block_len, block_len)]
    firsts = [1] + ends[:-1]
    return [(a, b - a, n % 2) for n, (a, b) in enumerate(zip(firsts, ends)) if b > a]


even, last, offset_moved, end_moved = range(4)


def kind_of(slab):
    return (slab // block_len) & 1


def flag(flags_ref, which, like):
    return jnp.broadcast_to(flags_ref[which : which + 1, :], like.shape) != 0


def call(kernel, out_shapes, *args, result_outside=False, scratch=()):
    size = sum(4 * a.size for a in args) + sum(4 * o.size for o in out_shapes)
    return pl.pallas_call(
        kernel,
        out_shape=tuple(out_shapes),
        in_specs=[pl.BlockSpec(memory_space=pltpu.VMEM)] * len(args),
        out_specs=tuple(pl.BlockSpec(memory_space=pl.ANY if result_outside else pltpu.VMEM) for _ in out_shapes),
        scratch_shapes=list(scratch),
        compiler_params=pltpu.CompilerParams(vmem_limit_bytes=vmem_bytes),
        cost_estimate=pl.CostEstimate(flops=10 * size, bytes_accessed=size, transcendentals=0),
    )(*args)


def shape(*dims):
    return jax.ShapeDtypeStruct(dims, jnp.float32)


def plane_sum(x):
    rows, cols = x.shape[-2], x.shape[-1]
    total = pltpu.roll(x, 1, x.ndim - 2) + pltpu.roll(x, rows - 1, x.ndim - 2)
    total = total + pltpu.roll(x, 1, x.ndim - 1) + pltpu.roll(x, cols - 1, x.ndim - 1)
    return total - 6.0 * x


def reactions(s, c):
    product = s * c * c
    return feed_rate * (1.0 - s) - product, product - (feed_rate + kill_rate) * c


def plane_rates(lo, middle, hi):
    lap = [plane_sum(middle[f]) + lo[f] + hi[f] for f in range(2)]
    react = reactions(*middle)
    return [diffuse[f] * lap[f] + react[f] for f in range(2)]


def put_edges(flags_ref, far_ref, near_ref, at, head, tail):
    here = flag(flags_ref, even, head)
    far_ref[at] = jnp.where(here, head, tail)
    near_ref[at] = jnp.where(here, tail, head)


def below(flags_ref, far, near):
    return jnp.where(flag(flags_ref, even, far), far, near)


def above(flags_ref, far, near):
    return jnp.where(flag(flags_ref, even, far), near, far)


def combined(states_ref, way, f, p):
    w = old_weights[way]
    return sum(w[j] * states_ref[j, f, p] for j in range(3))


def start_kernel(flags_ref, states_ref, first_edges_ref, far_ref, near_ref):
    sides = (0, states_ref.shape[2] - 1)
    for f in range(2):
        for way in range(2):
            put_edges(flags_ref, far_ref, near_ref, (way, f), *[combined(states_ref, way, f, p) for p in sides])
        ends = [states_ref[2, f, p] for p in sides]
        ends = [jnp.where(flag(flags_ref, last, x), first_edges_ref[f, e], x) for e, x in enumerate(ends)]
        put_edges(flags_ref, far_ref, near_ref, (2, f), *ends)


def old_kernel(flags_ref, states_ref, first_ref, part_ref, start_ref):
    depth = states_ref.shape[2]
    for p in range(depth):
        for f in range(2):
            own = states_ref[2, f, p]
            start_ref[f, p] = jnp.where(flag(flags_ref, last, own), first_ref[f, p], own)
        react = [reactions(states_ref[j, 0, p], states_ref[j, 1, p]) for j in range(3)]
        for way in range(2):
            for f in range(2):
                middle = combined(states_ref, way, f, p)
                total = plane_sum(middle)
                if p > 0:
                    total = total + combined(states_ref, way, f, p - 1)
                if p < depth - 1:
                    total = total + combined(states_ref, way, f, p + 1)
                part = diffuse[f] * total
                for j in range(3):
                    part = part + old_weights[way][j] * react[j][f]
                part_ref[way, f, p] = part


def sum_kernel(flags_ref, part_ref, far_ref, near_ref, *out_refs):
    depth = part_ref.shape[2]
    for way, out_ref in enumerate(out_refs):
        for f in range(2):
            for p in range(depth):
                total = part_ref[way, f, p]
                if p == 0:
                    total = total + diffuse[f] * below(flags_ref, far_ref[way, f], near_ref[way, f])
                if p == depth - 1:
                    total = total + diffuse[f] * above(flags_ref, far_ref[way, f], near_ref[way, f])
                out_ref[f, p] = total


def planes_with(flags_ref, x_ref, far_ref, near_ref):
    depth = x_ref.shape[1]

    def plane(p):
        if p < 0:
            return [below(flags_ref, far_ref[f], near_ref[f]) for f in range(2)]
        if p >= depth:
            return [above(flags_ref, far_ref[f], near_ref[f]) for f in range(2)]
        return [x_ref[f, p] for f in range(2)]

    return plane


def node_kernel(way, flags_ref, old_ref, x_ref, far_ref, near_ref, *refs):
    depth = x_ref.shape[1]
    plane = planes_with(flags_ref, x_ref, far_ref, near_ref)
    if way == 0:
        next_ref, keep_ref, next_far_ref, next_near_ref = refs
    else:
        rate_ref, next_ref, keep_ref, next_far_ref, next_near_ref = refs
    for p in range(depth):
        rate = plane_rates(plane(p - 1), plane(p), plane(p + 1))
        for f in range(2):
            next_ref[f, p] = x_ref[f, p] + half_step * rate[f] + old_ref[f, p]
            if way == 0:
                keep_ref[f, p] = rate[f]
            else:
                keep_ref[f, p] = new_weights[0] * rate_ref[f, p] + new_weights[1] * rate[f]
    for f in range(2):
        put_edges(flags_ref, next_far_ref, next_near_ref, f, next_ref[f, 0], next_ref[f, depth - 1])


def offset_kernel(
    count, flags_ref, x_ref, far_ref, near_ref, sum_ref, start_ref, node_ref, rate_ref,
    send_ref, offset_ref, mid_ref,
):
    depth = x_ref.shape[1]
    plane = planes_with(flags_ref, x_ref, far_ref, near_ref)
    for p in range(depth):
        rate = plane_rates(plane(p - 1), plane(p), plane(p + 1))
        for f in range(2):
            offset = sum_ref[f, p] + new_weights[2] * rate[f]
            offset_ref[f, p] = offset
            first = start_ref[f, p] + step_time * rate_ref[f, p] + offset
            offset = jnp.where(flag(flags_ref, last, offset), first, offset)
            moved = pltpu.roll(offset, half_rows, 0), pltpu.roll(offset, rows_each, 0)
            offset = jnp.where(flag(flags_ref, offset_moved, offset), *moved)
            offset = jnp.concatenate([offset, offset[: 2 * rows_each]], axis=0)
            place = rows_sent * p
            shift = (place - 1) % rows_each
            if shift:
                offset = pltpu.roll(offset, shift, 0)
            for i in range(count):
                start = rank_of(i, count) * rows_each + 1 + shift
                send_ref[i, f, place : place + rows_sent] = offset[start : start + rows_sent]
            mid_ref[f, p] = node_ref[f, p] - 0.5 * (start_ref[f, p] + x_ref[f, p])


def edge_lists(steps):
    return [(0, steps)] + [(j, steps - j) for j in range(1, steps)]


def joined(kind, own, come):
    return jnp.concatenate([come, own] if kind == 0 else [own, come], axis=-2)


def unpacked(ref, lead, at, first):
    kept = 2 * rows_each
    start = min(max(at - first, 0), ref.shape[-2] - kept)
    rows = ref[(*lead, slice(start, start + kept))]
    shift = (start + first - at) % kept
    return pltpu.roll(rows, shift, 0) if shift else rows


def rows_of(kind, state, offsets_ref):
    def plane(a, f, p):
        if a:
            return unpacked(offsets_ref, (a - 1, f), rows_sent * p, 1)
        if len(state) == 1:
            return unpacked(state[0], (f,), rows_sent * p, 1)
        return joined(kind, state[0][f, p], state[1][f, p])

    return plane


def edge_pieces(steps):
    pieces, at = [], 0
    for a, n in edge_lists(steps):
        for away in range(1, n + 1):
            around = half_rows if a == 0 and away == 1 else n - away
            first, end = half_rows - around, half_rows + rows_each + around
            pieces.append((a, away, at, first, end))
            at += end - first
    return pieces, -(-at // rows_each) * rows_each


def edge_kernel(kind, steps, flags_ref, offsets_ref, *refs):
    far_ref, near_ref = refs[-2:]
    depth = offsets_ref.shape[2] // rows_sent
    plane = rows_of(kind, refs[:-2], offsets_ref)
    pieces, total = edge_pieces(steps)
    used = 0
    for a, away, at, first, end in pieces:
        used = at + end - first
        for f in range(2):
            ends = plane(a, f, away - 1), plane(a, f, depth - away)
            put_edges(flags_ref, far_ref, near_ref, (f, slice(at, used)), *[x[first:end] for x in ends])
    if used < total:
        for f in range(2):
            for ref in (far_ref, near_ref):
                ref[f, used:total] = jnp.zeros((total - used, ref.shape[-1]), jnp.float32)


def block_kernel(kind, steps, flags_ref, offsets_ref, *refs):
    closing = refs[-1].shape[0] > steps
    far_ref, near_ref, out_ref, end_ref = (*refs[-3:], None) if closing else refs[-4:]
    depth = offsets_ref.shape[2] // rows_sent
    state = refs[: -3 if closing else -4]
    opening = len(state) == 1
    plane = rows_of(kind, state, offsets_ref)
    halos = {}
    for a, away, at, first, _ in edge_pieces(steps)[0]:
        halos.setdefault(a, []).append((at, first))

    def halo(f, piece, side):
        return side(flags_ref, *[unpacked(ref, (f,), *piece) for ref in (far_ref, near_ref)])

    def extended(a, f):
        planes = [plane(a, f, p) for p in range(depth)]
        pieces = halos.get(a, [])
        lo = [halo(f, piece, below) for piece in reversed(pieces)]
        hi = [halo(f, piece, above) for piece in pieces]
        return jnp.stack(lo + planes + hi)

    state = [extended(0, f) for f in range(2)]
    for f in range(2):
        before = state[f][steps - 1 : steps + depth + 1]
        if opening:
            out_ref[0, f] = pltpu.roll(before, 2 * rows_each - half_rows, 1)[:, :rows_each]
        else:
            out_ref[0, f] = before[:, rows_each:] if kind == 0 else before[:, :rows_each]
    for j in range(1, steps + 1):
        middle = [x[1:-1] for x in state]
        rate = plane_rates([x[:-2] for x in state], middle, [x[2:] for x in state])
        state = [middle[f] + step_time * rate[f] + extended(j, f) for f in range(2)]
        around = steps - j
        for f in range(2):
            if j < steps:
                inner = state[f][around - 1 : around + depth + 1]
                out_ref[j, f] = pltpu.roll(inner, 2 * rows_each - half_rows, 1)[:, :rows_each]
                continue
            end = pltpu.roll(state[f], 2 * rows_each - half_rows, 1)[:, :rows_each]
            if closing:
                out_ref[steps, f, 1 : depth + 1] = end
                for p in (0, depth + 1):
                    out_ref[steps, f, p] = jnp.zeros_like(end[0])
            else:
                end_ref[f] = end


def result_kernel(count, flags_ref, come_ref, offset_ref, mid_ref, out_hbm, out_ref, sems):
    depth = mid_ref.shape[1]

    def whole(f, p):
        full = jnp.concatenate([come_ref[index_of(r, count), f, p + 1] for r in range(count)], axis=0)
        return jnp.where(flag(flags_ref, end_moved, full), pltpu.roll(full, full.shape[0] - half_rows, 0), full)

    planes = [[whole(f, p) for f in range(2)] for p in range(-1, depth + 1)]
    copies = []
    for p in range(depth):
        here = planes[p + 1]
        rate = plane_rates(planes[p], here, planes[p + 2])
        for f in range(2):
            end = here[f] + step_time * rate[f] + offset_ref[f, p]
            middle = mid_ref[f, p] + 0.5 * (here[f] + end)
            newest = flag(flags_ref, last, end)
            out_ref[p, 0, f] = here[f]
            out_ref[p, 1, f] = jnp.where(newest, here[f], middle)
            out_ref[p, 2, f] = jnp.where(newest, here[f], end)
        copies.append(pltpu.make_async_copy(out_ref.at[p], out_hbm.at[0, :, :, p], sems.at[p]))
        copies[-1].start()
    for copy in copies:
        copy.wait()


def swapped(far, near):
    count = lax.axis_size("space")
    far = lax.ppermute(far, "space", [((i + j) % count, (i + 1 - j) % count) for i in range(1, count, 2) for j in range(2)])
    near = lax.ppermute(near, "space", [(i + j, i + 1 - j) for i in range(0, count, 2) for j in range(2)])
    return far, near


def local(states, first_start):
    count = lax.axis_size("tm")
    me = lax.axis_index("tm")
    blocks = chain_blocks(count)
    slab = states[0]
    _, _, depth, rows, cols = slab.shape
    grid = shape(2, depth, rows, cols)
    edge = shape(2, rows, cols)

    newest = me == count - 1
    flags = jnp.stack([
        lax.axis_index("space") & 1 == 0,
        newest,
        ~newest & (kind_of(me + 1) == 1),
        kind_of(me) == 0,
    ]).astype(jnp.int32)
    flags = jnp.broadcast_to(flags[:, None], (4, 128))

    back_one = [(i, (i - 1) % count) for i in range(count)]
    message = shape(3, 2, rows, cols)
    first_edges = first_start[:, :: depth - 1]
    far, near = call(start_kernel, [message] * 2, flags, slab, first_edges)
    far, near = swapped(far, near)
    part, fine0 = call(old_kernel, [shape(2, 2, depth, rows, cols), grid], flags, slab, first_start)
    old_first, old_second = call(sum_kernel, [grid] * 2, flags, part, far, near)
    old_first = lax.ppermute(old_first, "tm", back_one)
    old_second = lax.ppermute(old_second, "tm", back_one)

    fine1, rate0, far, near = call(
        functools.partial(node_kernel, 0), [grid] * 2 + [edge] * 2,
        flags, old_first, fine0, far[2], near[2],
    )
    far, near = swapped(far, near)
    fine2, total, far, near = call(
        functools.partial(node_kernel, 1), [grid] * 2 + [edge] * 2,
        flags, old_second, fine1, far, near, rate0,
    )
    far, near = swapped(far, near)
    send, offset, mid = call(
        functools.partial(offset_kernel, count),
        [shape(count, 2, depth * rows_sent, cols), grid, grid],
        flags, fine2, far, near, total, fine0, fine1, rate0,
    )
    held = lax.all_to_all(send, "tm", 0, 0, tiled=True)

    state = [held[count - 1]]
    ends = []
    for first, steps, kind in blocks:
        if ends:
            way = 1 if kind == 0 else -1
            route = [(index_of(r, count), index_of((r + way) % count, count)) for r in range(count)]
            state = [end[0], lax.ppermute(end[0], "tm", route)]
        offsets = held[first - 1 : first - 1 + steps]
        message = shape(2, edge_pieces(steps)[1], cols)
        far, near = call(functools.partial(edge_kernel, kind, steps), [message] * 2, flags, offsets, *state)
        far, near = swapped(far, near)
        closing = first + steps == count
        block, *end = call(
            functools.partial(block_kernel, kind, steps),
            [shape(steps + closing, 2, depth + 2, rows_each, cols)]
            + [shape(2, depth, rows_each, cols)] * (not closing),
            flags, offsets, *state, far, near,
        )
        ends.append(block)
    back = lax.all_to_all(jnp.concatenate(ends), "tm", 0, 0, tiled=True)
    (result,) = call(
        functools.partial(result_kernel, count), [shape(1, 3, 2, depth, rows, cols)], flags, back, offset, mid,
        result_outside=True,
        scratch=[pltpu.VMEM((depth, 3, 2, rows, cols), jnp.float32), pltpu.SemaphoreType.DMA((depth,))],
    )
    return result


def solution(mesh):
    return jax.shard_map(
        local,
        mesh=mesh,
        in_specs=(P("tm", None, None, "space", None, None), P(None, "space", None, None)),
        out_specs=P("tm", None, None, "space", None, None),
        check_vma=False,
    )
```
